32 devices in a mesh: groups: 2 (over y), dp: 4 (over x, core), tensor: 4 (over z).
Axes of the slice: x: 2, y: 2, z: 4, core: 2. Of those that a mesh axis runs over, the one named last changes fastest.
Arguments:
- tokens: bfloat16 [1, 64, 8192], P(None, 'groups', 'dp'), parts along dimension 1, may hold values from -6 to 6
- parents: int32 [1, 64], P(None, 'groups'), parts along dimension 1, may hold values from 0 to 31, as said below
- norm_gains: float32 [2, 8192], P(None, 'dp'), may hold values from 0.1 to 1.9
- weight_xz: bfloat16 [8192, 2, 8192], P('dp', None, 'tensor'), may hold values from -0.0625 to 0.0625
- weight_bc: bfloat16 [8192, 2, 1024], P('dp', None, 'tensor'), may hold values from -0.0625 to 0.0625
- weight_dt: bfloat16 [8192, 128], P('dp', 'tensor'), may hold values from -0.0625 to 0.0625
- conv_inner: float32 [4, 8192], P(None, 'tensor'), may hold values from -3 to 3
- conv_groups: float32 [4, 2, 1024], P(None, None, 'tensor'), may hold values from -3 to 3
- dt_bias: float32 [128], P('tensor'), may hold values from -3 to 1
- rates: float32 [128], P('tensor'), may hold values from 0.05 to 4
- skip_gain: float32 [128], P('tensor'), may hold values from 0.5 to 2
- gate_gain: float32 [8192], P('tensor'), may hold values from 0.1 to 1.9
- weight_out: bfloat16 [8192, 8192], P('tensor', 'dp'), may hold values from -0.0625 to 0.0625
- weight_up: bfloat16 [8192, 16384], P('dp', 'tensor'), may hold values from -0.0625 to 0.0625
- weight_down: bfloat16 [16384, 8192], P('tensor', 'dp'), may hold values from -0.046875 to 0.046875
- ssm_state: bfloat16 [64, 128, 64, 128], P(('groups', 'dp'), 'tensor'), parts along dimension 0, may hold values from -4 to 4
- queue_inner: bfloat16 [64, 3, 8192], P(('groups', 'dp'), None, 'tensor'), parts along dimension 0, may hold values from -6 to 6
- queue_groups: bfloat16 [64, 3, 2, 1024], P(('groups', 'dp'), None, None, 'tensor'), parts along dimension 0, may hold values from -6 to 6
Outputs:
- beam_out: bfloat16 [1, 64, 8192], P(None, 'groups', 'dp'), parts along dimension 1
- final_state: bfloat16 [64, 128, 64, 128], P(('groups', 'dp'), 'tensor'), parts along dimension 0
- final_inner: bfloat16 [64, 3, 8192], P(('groups', 'dp'), None, 'tensor'), parts along dimension 0
- final_groups: bfloat16 [64, 3, 2, 1024], P(('groups', 'dp'), None, None, 'tensor'), parts along dimension 0
The draws below stay inside these ranges and needn't reach their ends.
There are 2 independent parts, one for each index of `groups`. The reference program is written for one: setup_inputs(seed, part) draws one part's arguments, and reference() takes and returns one part's arrays. A program takes and returns all parts, laid end to end along the dimension named above; an argument that names none is the same for every part. Nothing has to cross between parts.
Inputs may be any that keep to these rules, and one draw needn't show every extreme that they name: At each step the 8 rows of one index of dp (rows i * 8 to (i + 1) * 8 - 1) take at most 4 parents from the rows of any one index of dp, its own included, and exactly 4 from some index.
All inputs are finite; a program needn't handle non-finite values.
Results may differ from the reference program's by a relative error of at most 0.01.
Values may be sent and summed in bfloat16 or wider, within the bound.
No kernel may reach another device: no remote copies, remote signals or barrier semaphores. Data moves between devices by JAX's collectives and lax.ppermute only.
A program may use at most 256 MiB of HBM per device.

```python
import math
import jax
import jax.numpy as jnp
from jax import lax

D = 8192
H = 128
P_SIZE = 64
N = 128
G = 8
FF = 16384
KC = 4
STEPS = 1
ROWS_DEV = 8
BEAMS = 32
CAP = 4


def draw_parents(key, part):
    key = jax.random.fold_in(key, 7)
    devices = BEAMS // ROWS_DEV

    def one_block(block_key):
        keys = jax.random.split(block_key, 4)
        crowded = jax.random.randint(keys[0], (), 0, devices).astype(jnp.int32)
        others = (jax.random.permutation(keys[1], (devices - 1) * CAP) // CAP).astype(jnp.int32)
        others = others + (others >= crowded).astype(jnp.int32)
        chosen = jnp.concatenate([jnp.full((CAP,), 1, jnp.int32) * crowded, others[:ROWS_DEV - CAP]])
        chosen = jax.random.permutation(keys[2], chosen)
        within = jax.random.randint(keys[3], (ROWS_DEV,), 0, ROWS_DEV).astype(jnp.int32)
        return chosen * ROWS_DEV + within
    block_keys = jax.random.split(key, STEPS * devices)
    return jax.vmap(one_block)(block_keys).reshape(STEPS, BEAMS).astype(jnp.int32)


def block_scale(rng, shape, cuts, least, top_value):
    level = 1.0
    for dim, blocks in cuts:
        heights = jax.random.uniform(jax.random.fold_in(jax.random.fold_in(rng, 6), dim), (blocks,), jnp.float32, least / len(cuts), top_value / len(cuts))
        level = level * jnp.repeat(jnp.exp(heights), shape[dim] // blocks).reshape((-1,) + (1,) * (len(shape) - 1 - dim))
    return level


def bell_draw(stream_key, extent, deviation, bound, shards=(), held_as=jnp.bfloat16):
    factor_of = block_scale(stream_key, extent, shards, -0.22, 0.18) if shards else 1.0
    result = jax.random.normal(stream_key, extent, jnp.float32) * deviation * factor_of
    return jnp.minimum(jnp.maximum(result, -bound), bound).astype(held_as)


def setup_inputs(seed: int = 0, part: int = 0) -> dict:
    seeds = jax.random.split(jax.random.key(seed), 19)
    part_splits = jax.random.split(jax.random.fold_in(seeds[18], part), 19)
    tokens = bell_draw(part_splits[0], (STEPS, BEAMS, D), 1.0, 6.0, ((2, 4),))
    parents = draw_parents(jax.random.fold_in(jax.random.fold_in(seeds[18], part), 71), part)
    norm_gains = jnp.clip(1.0 + 0.18 * jax.random.normal(seeds[2], (2, D), jnp.float32), 0.1, 1.9)
    weight_xz = bell_draw(seeds[3], (D, 2, H * P_SIZE), D ** -0.5, 0.0625, ((0, 4), (2, 4)))
    weight_bc = bell_draw(seeds[4], (D, 2, G * N), D ** -0.5, 0.0625, ((0, 4), (2, 4)))
    weight_dt = bell_draw(seeds[5], (D, H), D ** -0.5, 0.0625, ((0, 4), (1, 4)))
    conv_inner = bell_draw(seeds[6], (KC, H * P_SIZE), 0.5, 3.0, ((1, 4),), jnp.float32)
    conv_groups = bell_draw(seeds[7], (KC, 2, G * N), 0.5, 3.0, ((2, 4),), jnp.float32)
    dt_bias = jnp.clip(-3.0 + 4.0 * jax.random.uniform(seeds[8], (H,), jnp.float32) ** block_scale(seeds[8], (H,), ((0, 4),), -0.2, 0.2), -3.0, 1.0)
    rates = jnp.clip(jnp.exp(math.log(4.0) - 4.3820266 * jax.random.uniform(seeds[9], (H,), jnp.float32) ** block_scale(seeds[9], (H,), ((0, 4),), -0.2, 0.2)), 0.05, 4.0)
    skip_gain = jnp.clip(0.5 + 1.5 * jax.random.uniform(seeds[10], (H,), jnp.float32) ** block_scale(seeds[10], (H,), ((0, 4),), -0.2, 0.2), 0.5, 2.0)
    gate_gain = jnp.clip(1.0 + 0.18 * jax.random.normal(seeds[11], (H * P_SIZE,), jnp.float32), 0.1, 1.9)
    weight_out = bell_draw(seeds[12], (H * P_SIZE, D), (H * P_SIZE) ** -0.5, 0.0625, ((0, 4), (1, 4)))
    weight_up = bell_draw(seeds[13], (D, FF), D ** -0.5, 0.0625, ((0, 4), (1, 4)))
    weight_down = bell_draw(seeds[14], (FF, D), FF ** -0.5, 0.046875, ((0, 4), (1, 4)))
    ssm_state = bell_draw(part_splits[15], (BEAMS, H, P_SIZE, N), 0.5, 4.0, ((0, 4), (1, 4)))
    queue_inner = bell_draw(part_splits[16], (BEAMS, KC - 1, H * P_SIZE), 1.0, 6.0, ((0, 4), (2, 4)))
    queue_groups = bell_draw(part_splits[17], (BEAMS, KC - 1, 2, G * N), 1.0, 6.0, ((0, 4), (3, 4)))
    return dict(tokens=tokens, parents=parents, norm_gains=norm_gains, weight_xz=weight_xz, weight_bc=weight_bc, weight_dt=weight_dt, conv_inner=conv_inner, conv_groups=conv_groups, dt_bias=dt_bias, rates=rates, skip_gain=skip_gain, gate_gain=gate_gain, weight_out=weight_out, weight_up=weight_up, weight_down=weight_down, ssm_state=ssm_state, queue_inner=queue_inner, queue_groups=queue_groups)


epsilon = 1e-05

def row_update(packed):
    ssm_rows, decays, step_size, inner_vals, keys_b, keys_c = packed
    updated = decays[:, None, None] * ssm_rows.astype(jnp.float32) + (step_size[:, None] * inner_vals)[:, :, None] * keys_b[:, None, :]
    mixed_out = lax.optimization_barrier(jnp.sum(updated * keys_c[:, None, :], axis=-1))
    return (updated.astype(jnp.bfloat16), mixed_out)

def reference(tokens, parents, norm_gains, weight_xz, weight_bc, weight_dt, conv_inner, conv_groups, dt_bias, rates, skip_gain, gate_gain, weight_out, weight_up, weight_down, ssm_state, queue_inner, queue_groups):
    inner_width = H * P_SIZE
    group_width = G * N
    group_heads = H // G
    beam_count = tokens.shape[1]
    carried = ssm_state
    queue_one = queue_inner
    queue_two = queue_groups
    results = []
    for turn_index in range(STEPS):
        chosen = parents[turn_index]
        carried = carried[chosen]
        queue_one = queue_one[chosen]
        queue_two = queue_two[chosen]
        inputs = tokens[turn_index].astype(jnp.float32)
        scale_one = lax.rsqrt(lax.optimization_barrier(jnp.sum(inputs * inputs, axis=1)) / D + epsilon)
        normed = (inputs * scale_one[:, None] * norm_gains[0]).astype(jnp.bfloat16)
        proj_pair = jnp.dot(normed, weight_xz.reshape(D, 2 * inner_width), preferred_element_type=jnp.float32)
        proj_inner = proj_pair[:, :inner_width]
        proj_gate = proj_pair[:, inner_width:]
        proj_groups = jnp.dot(normed, weight_bc.reshape(D, 2 * group_width), preferred_element_type=jnp.float32).reshape(beam_count, 2, group_width)
        raw_steps = jnp.dot(normed, weight_dt, preferred_element_type=jnp.float32)
        window_one = jnp.concatenate([queue_one.astype(jnp.float32), proj_inner[:, None]], axis=1)
        conv_one = jax.nn.silu(lax.optimization_barrier(jnp.sum(window_one * conv_inner[None], axis=1)))
        window_two = jnp.concatenate([queue_two.astype(jnp.float32), proj_groups[:, None]], axis=1)
        conv_two = jax.nn.silu(lax.optimization_barrier(jnp.sum(window_two * conv_groups[None], axis=1)))
        queue_one = window_one[:, 1:].astype(jnp.bfloat16)
        queue_two = window_two[:, 1:].astype(jnp.bfloat16)
        step_size = jax.nn.softplus(raw_steps + dt_bias)
        decays = jnp.exp(-step_size * rates)
        inner_vals = conv_one.reshape(beam_count, H, P_SIZE)
        keys_b = jnp.repeat(conv_two[:, 0].reshape(beam_count, G, N), group_heads, axis=1)
        keys_c = jnp.repeat(conv_two[:, 1].reshape(beam_count, G, N), group_heads, axis=1)
        carried, mixed_out = lax.map(row_update, (carried, decays, step_size, inner_vals, keys_b, keys_c))
        mixed_out = mixed_out + skip_gain[None, :, None] * inner_vals
        gated = mixed_out.reshape(beam_count, inner_width) * jax.nn.silu(proj_gate)
        grouped = gated.reshape(beam_count, G, group_heads * P_SIZE)
        grouped = grouped * lax.rsqrt(lax.optimization_barrier(jnp.sum(grouped * grouped, axis=2, keepdims=True)) / (group_heads * P_SIZE) + epsilon)
        activity = (grouped.reshape(beam_count, inner_width) * gate_gain).astype(jnp.bfloat16)
        residual = inputs + jnp.dot(activity, weight_out, preferred_element_type=jnp.float32)
        scale_two = lax.rsqrt(lax.optimization_barrier(jnp.sum(residual * residual, axis=1)) / D + epsilon)
        normed_two = (residual * scale_two[:, None] * norm_gains[1]).astype(jnp.bfloat16)
        hidden = jnp.square(jax.nn.relu(jnp.dot(normed_two, weight_up, preferred_element_type=jnp.float32))).astype(jnp.bfloat16)
        results.append((residual + jnp.dot(hidden, weight_down, preferred_element_type=jnp.float32)).astype(jnp.bfloat16))
    return (jnp.stack(results), carried, queue_one, queue_two)
```

```python
import functools

import jax
import jax.numpy as jnp
from jax import lax
from jax.experimental import pallas as pl
from jax.experimental.pallas import tpu as pltpu
from jax.sharding import PartitionSpec as P

D = 8192
H = 128
G = 8
EPS = 1e-05
LANES = 128
MIB = 1 << 20

F32 = jnp.float32
BF16 = jnp.bfloat16

VM = pl.BlockSpec(memory_space=pltpu.VMEM)
SM = pl.BlockSpec(memory_space=pltpu.SMEM)
ANY = pl.BlockSpec(memory_space=pl.ANY)


def dot(a, b):
    return jnp.dot(a, b, preferred_element_type=F32)


def dot_t(a, b):
    return lax.dot_general(a, b, (((1,), (1,)), ((), ())), preferred_element_type=F32)


def iota(shape, dim):
    return lax.broadcasted_iota(jnp.int32, shape, dim)


def one_hot(condition):
    return jnp.where(condition, 1.0, 0.0).astype(BF16)


def split_two(value):
    high = value.astype(BF16)
    low = (value - high.astype(F32)).astype(BF16)
    return high, low


def call(kernel, outs, in_specs, args, vmem, name, scratch=(), out_specs=None, cost=None):
    single = not isinstance(outs, (list, tuple))
    if out_specs is None:
        out_specs = VM if single else [VM] * len(outs)
    return pl.pallas_call(
        kernel,
        out_shape=outs,
        in_specs=in_specs,
        out_specs=out_specs,
        scratch_shapes=list(scratch),
        name=name,
        cost_estimate=cost,
        compiler_params=pltpu.CompilerParams(vmem_limit_bytes=vmem),
    )(*args)


def shape_of(shape, dtype):
    return jax.ShapeDtypeStruct(shape, dtype)


def in_proj_kernel(heads, tok_ref, gain_ref, xz_ref, bc_ref, dt_ref, out_ref, xz_buf, bc_buf, lhs, dt_buf, sem, sem_bc):
    rows, depth = tok_ref.shape
    tiles = xz_buf.shape[0]
    tiles_bc = bc_buf.shape[0]
    inner = tiles * LANES
    groups_width = tiles_bc * LANES
    copies = [pltpu.make_async_copy(xz_ref.at[:, t], xz_buf.at[t], sem.at[t]) for t in range(tiles)]
    copies_bc = [pltpu.make_async_copy(bc_ref.at[:, t], bc_buf.at[t], sem_bc.at[t]) for t in range(tiles_bc)]
    for one in copies:
        one.start()
    for one in copies_bc:
        one.start()
    inputs = tok_ref[...].astype(F32)
    squares = jnp.sum(inputs * inputs, axis=1, keepdims=True)
    scaled = (inputs * gain_ref[0:1, :]).astype(BF16)
    row = iota((LANES, 2 * LANES), 0)
    col = iota((LANES, 2 * LANES), 1)
    even = one_hot(col == 2 * row)
    odd = one_hot(col == 2 * row + 1)
    for i in range(depth // LANES):
        block = scaled[:, i * LANES : (i + 1) * LANES]
        where = slice(i * 2 * LANES, (i + 1) * 2 * LANES)
        lhs[0:rows, where] = dot(block, even).astype(BF16)
        lhs[rows : 2 * rows, where] = dot(block, odd).astype(BF16)
    dt_buf[...] = jnp.zeros_like(dt_buf)
    dt_buf[0:heads, :] = dt_ref[...]
    tail = dot_t(scaled, dt_buf[...])
    high, low = split_two(squares)
    lane = iota(tail.shape, 1)
    tail = jnp.where(lane == heads, high.astype(F32), jnp.where(lane == heads + 1, low.astype(F32), tail))
    base = 2 * inner + 2 * groups_width
    out_ref[:, base : base + LANES] = tail.astype(BF16)

    def project(copies, view, start, width):
        count = len(copies)
        step = 2 if count % 2 == 0 else 1
        for t in range(0, count, step):
            for u in range(t, t + step):
                copies[u].wait()
            if step == 2:
                weights = jnp.concatenate([view[t], view[t + 1]], axis=1)
            else:
                weights = view[t]
            product = dot(lhs[...], weights).astype(BF16)
            at = start + t * LANES
            out_ref[:, at : at + step * LANES] = product[0:rows]
            out_ref[:, at + width : at + width + step * LANES] = product[rows : 2 * rows]

    project(copies, xz_buf.reshape(tiles, 2 * depth, LANES), 0, inner)
    project(copies_bc, bc_buf.reshape(tiles_bc, 2 * depth, LANES), 2 * inner, groups_width)


def in_proj(tokens, gains, weight_xz, weight_bc, weight_dt):
    rows, depth = tokens.shape
    inner = weight_xz.shape[2]
    groups_width = weight_bc.shape[2]
    heads = weight_dt.shape[1]
    tiles, tiles_bc = inner // LANES, groups_width // LANES
    xz = weight_xz.reshape(depth, 2, tiles, LANES).transpose(0, 2, 1, 3)
    bc = weight_bc.reshape(depth, 2, tiles_bc, LANES).transpose(0, 2, 1, 3)
    width = 2 * inner + 2 * groups_width + LANES
    return call(
        functools.partial(in_proj_kernel, heads),
        shape_of((rows, width), BF16),
        [VM, VM, ANY, ANY, VM],
        (tokens, gains, xz, bc, weight_dt.T),
        32 * MIB,
        "in_proj",
        scratch=[
            pltpu.VMEM((tiles, depth, 2, LANES), BF16),
            pltpu.VMEM((tiles_bc, depth, 2, LANES), BF16),
            pltpu.VMEM((2 * rows, 2 * depth), BF16),
            pltpu.VMEM((LANES, depth), BF16),
            pltpu.SemaphoreType.DMA((tiles,)),
            pltpu.SemaphoreType.DMA((tiles_bc,)),
        ],
    )


def pick_rows_kernel(slots, ids_ref, own_ref, other_ref, code_ref, *out_refs):
    total = (own_ref[...].astype(F32) + other_ref[...].astype(F32)).astype(BF16)
    rows = total.shape[0]
    slot = iota((slots, rows), 0)
    for i, out_ref in enumerate(out_refs):
        pick = one_hot(code_ref[...] == ids_ref[i] * slots + slot)
        out_ref[...] = dot(pick, total).astype(BF16)


def pick_rows(targets, own, other, code_row, slots):
    width = own.shape[1]
    count = targets.shape[0]
    return call(
        functools.partial(pick_rows_kernel, slots),
        [shape_of((slots, width), BF16)] * count,
        [SM, VM, VM, VM],
        (targets, own, other, code_row),
        8 * MIB,
        "pick_rows",
    )


def chip_sum_kernel(own_ref, other_ref, out_ref):
    out_ref[...] = (own_ref[...].astype(F32) + other_ref[...].astype(F32)).astype(BF16)


def chip_sum(own, other):
    return call(chip_sum_kernel, shape_of(own.shape, BF16), [VM, VM], (own, other), 4 * MIB, "chip_sum")


def mixer_kernel(
    parts,
    heads,
    ids_ref,
    code_ref,
    local_ref,
    *refs,
):
    part_refs = refs[:parts]
    (
        conv_ref,
        conv_bc_ref,
        bias_ref,
        rates_ref,
        skip_ref,
        gain_ref,
        queue_ref,
        queue_bc_ref,
        state_ref,
        act_ref,
        message_ref,
    ) = refs[parts:]
    slots = part_refs[0].shape[0]
    inner = gain_ref.shape[1]
    lags, local_rows, _ = queue_ref.shape
    groups_width = queue_bc_ref.shape[3]
    state_size = state_ref.shape[3]
    head_size = state_ref.shape[2]
    groups_here = groups_width // state_size
    per_group = inner // groups_here
    proj = part_refs[0][...].astype(F32)
    for ref in part_refs[1:]:
        proj = proj + ref[...].astype(F32)
    base_bc = 2 * inner
    base = base_bc + 2 * groups_width
    tail = proj[:, base : base + LANES]
    lane = iota(tail.shape, 1)
    squares = jnp.sum(jnp.where((lane == heads) | (lane == heads + 1), tail, 0.0), axis=1, keepdims=True)
    scale = lax.rsqrt(squares / D + EPS)
    slot = iota((slots, code_ref.shape[1]), 0)
    mine = code_ref[...] == ids_ref[0] * slots + slot
    valid = jnp.sum(jnp.where(mine, 1.0, 0.0), axis=1, keepdims=True)
    parent = jnp.sum(jnp.where(mine, local_ref[...], 0), axis=1, keepdims=True)
    pick = jnp.where((iota((slots, local_rows), 1) == parent) & (valid > 0.0), 1.0, 0.0).astype(BF16)

    now = proj[:, 0:inner] * scale
    gate = proj[:, inner : 2 * inner] * scale
    conv = now * conv_ref[lags : lags + 1, :]
    for k in range(lags):
        held = dot(pick, queue_ref[k])
        conv = conv + held * conv_ref[k : k + 1, :]
        if k > 0:
            message_ref[:, (k - 1) * inner : k * inner] = held.astype(BF16)
    message_ref[:, (lags - 1) * inner : lags * inner] = now.astype(BF16)
    inner_vals = conv * jax.nn.sigmoid(conv)
    at = lags * inner
    keys = []
    for j in range(2):
        start = base_bc + j * groups_width
        now_bc = proj[:, start : start + groups_width] * scale
        conv_bc = now_bc * conv_bc_ref[lags, j : j + 1, :]
        for k in range(lags):
            held = dot(pick, queue_bc_ref[k, j])
            conv_bc = conv_bc + held * conv_bc_ref[k, j : j + 1, :]
            if k > 0:
                to = at + ((k - 1) * 2 + j) * groups_width
                message_ref[:, to : to + groups_width] = held.astype(BF16)
        to = at + ((lags - 1) * 2 + j) * groups_width
        message_ref[:, to : to + groups_width] = now_bc.astype(BF16)
        keys.append(conv_bc * jax.nn.sigmoid(conv_bc))
    at = at + lags * 2 * groups_width

    raw = tail * scale + bias_ref[...]
    steps = jnp.maximum(raw, 0.0) + jnp.log1p(jnp.exp(-jnp.abs(raw)))
    decays = jnp.exp(-steps * rates_ref[...])
    spread = one_hot(iota((LANES, inner), 0) == iota((LANES, inner), 1) // head_size)

    def expand(value):
        high, low = split_two(value)
        return dot(high, spread) + dot(low, spread)

    steps_wide = expand(steps)
    decays_wide = expand(decays)
    skip_wide = expand(jnp.broadcast_to(skip_ref[...], (8, LANES)))[0:1]
    update = steps_wide * inner_vals
    message_ref[:, at : at + inner] = update.astype(BF16)
    at = at + inner
    message_ref[:, at : at + groups_width] = keys[0].astype(BF16)
    at = at + groups_width
    decay_high, decay_low = split_two(decays)
    message_ref[:, at : at + LANES] = decay_high
    message_ref[:, at + LANES : at + 2 * LANES] = decay_low

    for g in range(groups_here):
        lanes = slice(g * state_size, (g + 1) * state_size)
        wide = slice(g * per_group, (g + 1) * per_group)
        b_vals, c_vals = keys[0][:, lanes], keys[1][:, lanes]
        high, low = split_two(c_vals)
        c_both = jnp.concatenate([high, low], axis=0)
        mixed = jnp.zeros((slots, per_group), F32)
        first_head = g * (per_group // head_size)
        for r in range(local_rows):
            block = state_ref[r, first_head : first_head + per_group // head_size]
            both = dot_t(c_both, block.reshape(per_group, state_size))
            mixed = mixed + jnp.where(parent == r, both[0:slots] + both[slots : 2 * slots], 0.0)
        inside = jnp.sum(b_vals * c_vals, axis=1, keepdims=True)
        mixed = decays_wide[:, wide] * mixed + update[:, wide] * inside + skip_wide[:, wide] * inner_vals[:, wide]
        gated = mixed * (gate[:, wide] * jax.nn.sigmoid(gate[:, wide]))
        mean = jnp.sum(gated * gated, axis=1, keepdims=True) / per_group
        out = gated * lax.rsqrt(mean + EPS) * gain_ref[:, wide]
        act_ref[:, wide] = jnp.where(valid > 0.0, out, 0.0).astype(BF16)


def mixer(ids, code_row, local_row, parts, params, queue, queue_bc, state):
    conv, conv_bc, bias, rates, skip, gain = params
    slots = parts[0].shape[0]
    inner = gain.shape[0]
    lags = queue.shape[0]
    groups_width = queue_bc.shape[3]
    heads = bias.shape[0]
    message = lags * (inner + 2 * groups_width) + inner + groups_width + 2 * LANES

    def lane_row(vector):
        return jnp.pad(vector, (0, LANES - heads)).reshape(1, LANES)

    return call(
        functools.partial(mixer_kernel, len(parts), heads),
        [shape_of((slots, inner), BF16), shape_of((slots, message), BF16)],
        [SM, VM, VM] + [VM] * len(parts) + [VM] * 9,
        (ids, code_row, local_row, *parts, conv, conv_bc, lane_row(bias), lane_row(rates), lane_row(skip), gain.reshape(1, inner), queue, queue_bc, state),
        12 * MIB,
        "mixer",
    )


def deal_kernel(capacity, ids_ref, message_ref, *out_refs):
    slots = message_ref.shape[0]
    count = len(out_refs)
    row = iota((slots, slots), 0)
    want = row
    for i in range(count):
        want = jnp.where(row // capacity == i, ids_ref[i] * capacity + row % capacity, want)
    order = one_hot(iota((slots, slots), 1) == want)
    dealt = dot(order, message_ref[...])
    for i, out_ref in enumerate(out_refs):
        out_ref[...] = dealt[i * capacity : (i + 1) * capacity].astype(BF16)


def deal(targets, message, capacity):
    count = targets.shape[0]
    return call(
        functools.partial(deal_kernel, capacity),
        [shape_of((capacity, message.shape[1]), BF16)] * count,
        [SM, VM],
        (targets, message),
        8 * MIB,
        "deal",
    )


def collect_kernel(capacity, slots, lags, groups_width, ids_ref, code_ref, *refs):
    in_refs, (inner_ref, groups_ref, update_ref, keys_ref, decay_ref) = refs[:-5], refs[-5:]
    rows = code_ref.shape[0]
    count = len(in_refs)
    inner = update_ref.shape[1]
    me = ids_ref[0]
    held = jnp.concatenate([ref[...].astype(F32) for ref in in_refs], axis=0).astype(BF16)
    col = iota((rows, count * capacity), 1)
    want = jnp.full(col.shape, -1, jnp.int32)
    for i in range(count):
        want = jnp.where(col // capacity == i, ids_ref[i] * slots + me * capacity + col % capacity, want)
    mine = dot(one_hot(code_ref[...] == want), held)
    for k in range(lags):
        inner_ref[k] = mine[:, k * inner : (k + 1) * inner].astype(BF16)
    at = lags * inner
    for k in range(lags):
        for j in range(2):
            start = at + (2 * k + j) * groups_width
            groups_ref[k, j] = mine[:, start : start + groups_width].astype(BF16)
    at = at + 2 * lags * groups_width
    update_ref[...] = mine[:, at : at + inner]
    at = at + inner
    keys_ref[...] = mine[:, at : at + groups_width]
    at = at + groups_width
    decay_ref[...] = mine[:, at : at + LANES] + mine[:, at + LANES : at + 2 * LANES]


def collect(sources, own_code, messages, slots, inner, groups_width, lags):
    capacity = messages[0].shape[0]
    rows = own_code.shape[0]
    return call(
        functools.partial(collect_kernel, capacity, slots, lags, groups_width),
        [
            shape_of((lags, rows, inner), BF16),
            shape_of((lags, 2, rows, groups_width), BF16),
            shape_of((rows, inner), F32),
            shape_of((rows, groups_width), F32),
            shape_of((rows, LANES), F32),
        ],
        [SM, VM] + [VM] * len(messages),
        (sources, own_code, *messages),
        8 * MIB,
        "collect",
    )


def update_kernel(sources, own_parents_ref, ids_ref, *refs):
    state_refs = refs[:sources]
    update_ref, keys_ref, decay_ref, out_ref, held, made, sem_in, sem_out = refs[sources:]
    rows, heads, head_size, state_size = held.shape
    local_rows = rows
    inner = update_ref.shape[1]
    groups_here = keys_ref.shape[1] // state_size
    per_group = inner // groups_here
    heads_group = heads // groups_here

    def fetch(j):
        parent = own_parents_ref[j]
        owner = parent // local_rows
        row = lax.rem(parent, local_rows)
        for i in range(sources):

            @pl.when(owner == ids_ref[i])
            def _(i=i):
                pltpu.make_async_copy(state_refs[i].at[row], held.at[j], sem_in.at[j]).start()

    for j in range(rows):
        fetch(j)
    spread = one_hot(iota((LANES, inner), 0) == iota((LANES, inner), 1) // head_size)
    high, low = split_two(decay_ref[...])
    decay_high, decay_low = dot(high, spread), dot(low, spread)
    columns = []
    for g in range(groups_here):
        wide = slice(g * per_group, (g + 1) * per_group)
        stacked = jnp.concatenate([update_ref[:, wide], decay_high[:, wide], decay_low[:, wide]], axis=0)
        columns.append(jnp.transpose(stacked).astype(BF16))
    row_id = iota((3 * rows, state_size), 0)
    for j in range(rows):
        pltpu.make_async_copy(state_refs[0].at[0], held.at[j], sem_in.at[j]).wait()
        for g in range(groups_here):
            keys = keys_ref[j : j + 1, g * state_size : (g + 1) * state_size]
            right_keys = jnp.where(row_id == j, keys, 0.0)
            right_ones = jnp.where((row_id == rows + j) | (row_id == 2 * rows + j), 1.0, 0.0)
            right = jnp.concatenate([right_keys, right_ones], axis=1).astype(BF16)
            both = dot(columns[g], right)
            which = slice(g * heads_group, (g + 1) * heads_group)
            before = held[j, which].reshape(per_group, state_size).astype(F32)
            after = both[:, state_size:] * before + both[:, :state_size]
            made[j, which] = after.astype(BF16).reshape(heads_group, head_size, state_size)
        pltpu.make_async_copy(made.at[j], out_ref.at[j], sem_out.at[j]).start()
    for j in range(rows):
        pltpu.make_async_copy(made.at[j], out_ref.at[j], sem_out.at[j]).wait()


def update_state(own_parents, ids, states, update, keys, decay):
    shape = states[0].shape
    return call(
        functools.partial(update_kernel, len(states)),
        shape_of(shape, BF16),
        [SM, SM] + [ANY] * len(states) + [VM] * 3,
        (own_parents, ids, *states, update, keys, decay),
        24 * MIB,
        "update_state",
        scratch=[
            pltpu.VMEM(shape, BF16),
            pltpu.VMEM(shape, BF16),
            pltpu.SemaphoreType.DMA((shape[0],)),
            pltpu.SemaphoreType.DMA((shape[0],)),
        ],
        out_specs=ANY,
    )


def out_proj_kernel(slots, ids_ref, code_ref, *refs):
    act_refs, (weight_ref, out_ref) = refs[:-2], refs[-2:]
    rows = code_ref.shape[0]
    count = len(act_refs)
    col = iota((rows, count * slots), 1)
    want = jnp.full(col.shape, -1, jnp.int32)
    for i in range(count):
        want = jnp.where(col // slots == i, ids_ref[i] * slots + col % slots, want)
    held = jnp.concatenate([ref[...] for ref in act_refs], axis=0)
    activity = dot(one_hot(code_ref[...] == want), held).astype(BF16)
    out_ref[...] = dot(activity, weight_ref[...]).astype(BF16)


def out_proj(sources, code_col, acts, weight):
    rows = code_col.shape[0]
    return call(
        functools.partial(out_proj_kernel, acts[0].shape[0]),
        shape_of((rows, weight.shape[1]), BF16),
        [SM, VM] + [VM] * (len(acts) + 1),
        (sources, code_col, *acts, weight),
        12 * MIB,
        "out_proj",
    )


def up_kernel(parts, tok_ref, gain_ref, *refs):
    part_refs = refs[:parts]
    weight_ref, residual_ref, out_ref = refs[parts:]
    residual = tok_ref[...].astype(F32)
    total = part_refs[0][...].astype(F32)
    for ref in part_refs[1:]:
        total = total + ref[...].astype(F32)
    residual = residual + total
    residual_ref[...] = residual
    squares = jnp.sum(residual * residual, axis=1, keepdims=True)
    scaled = (residual * gain_ref[1:2, :]).astype(BF16)
    width = weight_ref.shape[1]
    high, low = split_two(squares)
    lane = iota((scaled.shape[0], LANES), 1)
    out_ref[:, width : width + LANES] = jnp.where(
        lane == 0, high.astype(F32), jnp.where(lane == 1, low.astype(F32), 0.0)
    ).astype(BF16)
    out_ref[:, 0:width] = dot(scaled, weight_ref[...]).astype(BF16)


def up_proj(tokens, gains, parts, weight):
    rows, width = tokens.shape
    return call(
        functools.partial(up_kernel, len(parts)),
        [shape_of((rows, width), F32), shape_of((rows, weight.shape[1] + LANES), BF16)],
        [VM] * (len(parts) + 3),
        (tokens, gains, *parts, weight),
        20 * MIB,
        "up_proj",
    )


def down_kernel(*refs):
    part_refs, (weight_ref, out_ref) = refs[:-2], refs[-2:]
    total = part_refs[0][...].astype(F32)
    for ref in part_refs[1:]:
        total = total + ref[...].astype(F32)
    width = weight_ref.shape[0]
    squares = jnp.sum(total[:, width : width + LANES], axis=1, keepdims=True)
    hidden = jnp.maximum(total[:, 0:width] * lax.rsqrt(squares / D + EPS), 0.0)
    out_ref[...] = dot((hidden * hidden).astype(BF16), weight_ref[...]).astype(BF16)


def down_proj(parts, weight):
    rows = parts[0].shape[0]
    return call(
        down_kernel,
        shape_of((rows, weight.shape[1]), BF16),
        [VM] * (len(parts) + 1),
        (*parts, weight),
        20 * MIB,
        "down_proj",
    )


def finish_kernel(residual_ref, *refs):
    part_refs, out_ref = refs[:-1], refs[-1]
    total = part_refs[0][...].astype(F32)
    for ref in part_refs[1:]:
        total = total + ref[...].astype(F32)
    out_ref[0] = (residual_ref[...] + total).astype(BF16)


def finish(residual, parts):
    return call(
        finish_kernel,
        shape_of((1, *residual.shape), BF16),
        [VM] * (len(parts) + 1),
        (residual, *parts),
        6 * MIB,
        "finish",
    )


def on_device(
    tokens,
    parents,
    norm_gains,
    weight_xz,
    weight_bc,
    weight_dt,
    conv_inner,
    conv_groups,
    dt_bias,
    rates,
    skip_gain,
    gate_gain,
    weight_out,
    weight_up,
    weight_down,
    ssm_state,
    queue_inner,
    queue_groups,
):
    devices = lax.axis_size("dp")
    chips = devices // 2
    ranks = lax.axis_size("tensor")
    me = lax.axis_index("dp")
    chip, core = me // 2, me % 2
    local_rows = ssm_state.shape[0]
    lags = queue_inner.shape[1]
    inner = queue_inner.shape[2]
    groups_width = queue_groups.shape[3]
    capacity = max(2, 2 * local_rows // devices)
    slots = devices * capacity
    rows = parents.shape[1]
    barrier = lax.optimization_barrier

    def to_dp(value, hop, flip):
        pairs = [(i, ((i // 2 + hop) % chips) * 2 + ((i % 2) ^ flip)) for i in range(devices)]
        return lax.ppermute(value, "dp", pairs)

    def over_tensor(value):
        return [value] + [
            lax.ppermute(value, "tensor", [(i, (i + s) % ranks) for i in range(ranks)]) for s in range(1, ranks)
        ]

    hops = [(hop, flip) for hop in range(chips) for flip in range(2)]
    sources = jnp.stack([((chip + chips - hop) % chips) * 2 + (core ^ flip) for hop, flip in hops]).astype(jnp.int32)
    targets = jnp.stack([((chip + hop) % chips) * 2 + (core ^ flip) for hop, flip in hops]).astype(jnp.int32)

    chosen = parents[0]
    owner = chosen // local_rows
    place = jnp.arange(rows, dtype=jnp.int32)
    block = place // local_rows
    earlier = (owner[:, None] == owner[None, :]) & (block[:, None] == block[None, :]) & (place[None, :] < place[:, None])
    rank = jnp.sum(earlier, axis=1).astype(jnp.int32)
    code = owner * slots + block * capacity + rank
    code_row, code_col = code.reshape(1, rows), code.reshape(rows, 1)
    local_row = (chosen % local_rows).reshape(1, rows)
    own_code = lax.dynamic_slice_in_dim(code_col, me * local_rows, local_rows, 0)
    own_parents = lax.dynamic_slice_in_dim(chosen, me * local_rows, local_rows, 0)

    sibling_state = to_dp(ssm_state, 0, 1)
    far = {}
    for hop in range(1, chips):
        far[hop, 0] = to_dp(ssm_state, hop, 0)
        far[hop, 1] = to_dp(far[hop, 0], 0, 1)

    partial = in_proj(tokens[0], norm_gains, weight_xz, weight_bc, weight_dt)
    near = to_dp(partial, 0, 1)
    same_core = targets[0::2]
    picked = pick_rows(same_core, partial, near, code_row, slots)
    parts = [picked[0]] + [to_dp(picked[hop], hop, 0) for hop in range(1, chips)]
    act, message = mixer(
        sources,
        code_row,
        local_row,
        parts,
        (conv_inner, conv_groups, dt_bias, rates, skip_gain, gate_gain),
        queue_inner.transpose(1, 0, 2),
        queue_groups.transpose(1, 2, 0, 3),
        ssm_state,
    )
    acts = [act] + [to_dp(act, hop, flip) for hop, flip in hops[1:]]
    out_part = out_proj(sources, code_col, acts, weight_out)
    residual, up_part = up_proj(tokens[0], norm_gains, over_tensor(out_part), weight_up)
    up_chip = chip_sum(up_part, to_dp(up_part, 0, 1))
    down_part = down_proj([up_chip] + [to_dp(up_chip, hop, 0) for hop in range(1, chips)], weight_down)
    beam_out = finish(residual, over_tensor(down_part))

    dealt = deal(targets, message, capacity)
    messages = [dealt[0]] + [to_dp(dealt[i], *hops[i]) for i in range(1, devices)]
    final_inner, final_groups, update, keys, decay = collect(
        sources, own_code, messages, slots, inner, groups_width, lags
    )
    states = [ssm_state, sibling_state] + [far[hop, flip] for hop, flip in hops[2:]]
    final_state = update_state(own_parents, sources, states, update, keys, decay)
    return (beam_out, final_state, final_inner.transpose(1, 0, 2), final_groups.transpose(2, 0, 1, 3))


def solution(mesh):
    in_specs = (
        P(None, "groups", "dp"),
        P(None, "groups"),
        P(None, "dp"),
        P("dp", None, "tensor"),
        P("dp", None, "tensor"),
        P("dp", "tensor"),
        P(None, "tensor"),
        P(None, None, "tensor"),
        P("tensor"),
        P("tensor"),
        P("tensor"),
        P("tensor"),
        P("tensor", "dp"),
        P("dp", "tensor"),
        P("tensor", "dp"),
        P(("groups", "dp"), "tensor", None, None),
        P(("groups", "dp"), None, "tensor"),
        P(("groups", "dp"), None, None, "tensor"),
    )
    out_specs = (
        P(None, "groups", "dp"),
        P(("groups", "dp"), "tensor", None, None),
        P(("groups", "dp"), None, "tensor"),
        P(("groups", "dp"), None, None, "tensor"),
    )
    return jax.shard_map(
        on_device, mesh=mesh, in_specs=in_specs, out_specs=out_specs, check_vma=False
    )
```

```python
import functools

import jax
import jax.numpy as jnp
from jax import lax
from jax.experimental import pallas as pl
from jax.experimental.pallas import tpu as pltpu
from jax.sharding import PartitionSpec as P

D = 8192
H = 128
G = 8
EPS = 1e-05
LANES = 128
MIB = 1 << 20

F32 = jnp.float32
BF16 = jnp.bfloat16

VM = pl.BlockSpec(memory_space=pltpu.VMEM)
SM = pl.BlockSpec(memory_space=pltpu.SMEM)
ANY = pl.BlockSpec(memory_space=pl.ANY)


def dot(a, b):
    return jnp.dot(a, b, preferred_element_type=F32)


def dot_t(a, b):
    return lax.dot_general(a, b, (((1,), (1,)), ((), ())), preferred_element_type=F32)


def iota(shape, dim):
    return lax.broadcasted_iota(jnp.int32, shape, dim)


def one_hot(condition):
    return jnp.where(condition, 1.0, 0.0).astype(BF16)


def codes(parents_ref, local_rows, capacity, slots):
    rows = parents_ref.shape[1]
    parents = parents_ref[...]
    one, other = iota((rows, rows), 0), iota((rows, rows), 1)
    across = jnp.broadcast_to(parents, (rows, rows))
    down = jnp.sum(jnp.where(one == other, across, 0), axis=1, keepdims=True)
    same = (across // local_rows == down // local_rows) & (one // local_rows == other // local_rows)
    rank_row = jnp.sum(jnp.where(same & (one < other), 1, 0), axis=0, keepdims=True)
    rank_col = jnp.sum(jnp.where(same & (other < one), 1, 0), axis=1, keepdims=True)
    code_row = parents // local_rows * slots + iota((1, rows), 1) // local_rows * capacity + rank_row
    code_col = down // local_rows * slots + iota((rows, 1), 0) // local_rows * capacity + rank_col
    return code_row, code_col


def in_hbm(value):
    return pltpu.with_memory_space_constraint(value, pltpu.HBM)


def in_vmem(value):
    return pltpu.with_memory_space_constraint(value, pltpu.VMEM)


def split_two(value):
    high = value.astype(BF16)
    low = (value - high.astype(F32)).astype(BF16)
    return high, low


def call(kernel, outs, in_specs, args, vmem, name, scratch=(), out_specs=None, cost=None):
    single = not isinstance(outs, (list, tuple))
    if out_specs is None:
        out_specs = VM if single else [VM] * len(outs)
    return pl.pallas_call(
        kernel,
        out_shape=outs,
        in_specs=in_specs,
        out_specs=out_specs,
        scratch_shapes=list(scratch),
        name=name,
        cost_estimate=cost,
        compiler_params=pltpu.CompilerParams(vmem_limit_bytes=vmem),
    )(*args)


def shape_of(shape, dtype):
    return jax.ShapeDtypeStruct(shape, dtype)


def first_rows_kernel(ids_ref, parents_ref, state_ref, *refs):
    out_refs, sem = refs[:-1], refs[-1]
    local_rows = state_ref.shape[0]
    both = 2 * local_rows
    me = ids_ref[0]
    copies = []
    for hop, out_ref in enumerate(out_refs, 1):
        to = ids_ref[2 * hop] // 2
        low = jnp.int32(local_rows)
        for i in range(both):
            parent = parents_ref[0, to * both + i]
            here = parent // local_rows == me
            low = jnp.where(here, jnp.minimum(low, lax.rem(parent, local_rows)), low)
        row = jnp.where(low < local_rows, low, 0)
        copies.append(pltpu.make_async_copy(state_ref.at[pl.ds(row, 1)], out_ref, sem.at[hop - 1]))
        copies[-1].start()
    for copy in copies:
        copy.wait()


def first_rows(targets, parents, state):
    count = targets.shape[0] // 2 - 1
    return call(
        first_rows_kernel,
        [pltpu.VMEM((1, *state.shape[1:]), BF16)] * count,
        [SM, SM, ANY],
        (targets, parents, in_hbm(state)),
        MIB,
        "first_rows",
        scratch=[pltpu.SemaphoreType.DMA((count,))],
    )


def in_load_kernel(
    tok_hbm, gain_hbm, dt_hbm, xz_hbm, lhs_ref, tail_ref, piece_ref, tok_ref, gain_ref, dt_ref, sem_small, sem
):
    rows, depth = tok_ref.shape
    heads = dt_hbm.shape[0]
    small = [
        pltpu.make_async_copy(tok_hbm, tok_ref, sem_small.at[0]),
        pltpu.make_async_copy(gain_hbm, gain_ref, sem_small.at[1]),
        pltpu.make_async_copy(dt_hbm, dt_ref.at[pl.ds(0, heads)], sem_small.at[2]),
    ]
    copies = [pltpu.make_async_copy(xz_hbm.at[:, t], piece_ref.at[t], sem.at[t]) for t in range(piece_ref.shape[0])]
    for one in small + copies:
        one.start()
    dt_ref[heads:, :] = jnp.zeros((LANES - heads, depth), BF16)
    small[0].wait()
    small[1].wait()
    inputs = tok_ref[...].astype(F32)
    squares = jnp.sum(inputs * inputs, axis=1, keepdims=True)
    scaled = (inputs * gain_ref[0:1, :]).astype(BF16)
    row = iota((LANES, 4 * LANES), 0)
    col = iota((LANES, 4 * LANES), 1)
    spread = one_hot((col == 2 * row) | (col == 2 * LANES + 2 * row + 1))
    blocks = depth // LANES
    stacked = jnp.concatenate([scaled[:, i * LANES : (i + 1) * LANES] for i in range(blocks)], axis=0)
    wide = dot(stacked, spread).astype(BF16)
    for i in range(blocks):
        where = slice(i * 2 * LANES, (i + 1) * 2 * LANES)
        block = wide[i * rows : (i + 1) * rows]
        lhs_ref[0:rows, where] = block[:, : 2 * LANES]
        lhs_ref[rows : 2 * rows, where] = block[:, 2 * LANES :]
    small[2].wait()
    tail = dot_t(scaled, dt_ref[...])
    high, low = split_two(squares)
    lane = iota(tail.shape, 1)
    tail = jnp.where(lane == heads, high.astype(F32), jnp.where(lane == heads + 1, low.astype(F32), tail))
    tail_ref[...] = tail.astype(BF16)
    for one in copies:
        one.wait()


def multiply_tiles(lhs, tiles_ref, store):
    count = tiles_ref.shape[0]
    step = 2 if count % 2 == 0 else 1
    for t in range(0, count, step):
        weights = tiles_ref[t] if step == 1 else jnp.concatenate([tiles_ref[t], tiles_ref[t + 1]], axis=1)
        store(t * LANES, step * LANES, dot(lhs, weights).astype(BF16))


def in_middle_kernel(lhs_ref, tiles_ref, xz_hbm, bc_hbm, out_ref, piece_ref, piece_bc_ref, sem, sem_bc):
    done = tiles_ref.shape[0]
    copies = [
        pltpu.make_async_copy(xz_hbm.at[:, done + t], piece_ref.at[t], sem.at[t]) for t in range(piece_ref.shape[0])
    ] + [pltpu.make_async_copy(bc_hbm.at[:, t], piece_bc_ref.at[t], sem_bc.at[t]) for t in range(piece_bc_ref.shape[0])]
    for one in copies:
        one.start()

    def store(start, width, product):
        out_ref[:, start : start + width] = product

    multiply_tiles(lhs_ref[...], tiles_ref, store)
    for one in copies:
        one.wait()


def in_last_kernel(lhs_ref, early_ref, tail_ref, tiles_ref, tiles_bc_ref, out_ref):
    rows = tail_ref.shape[0]
    before = early_ref.shape[1]
    inner = before + tiles_ref.shape[0] * LANES
    groups_width = tiles_bc_ref.shape[0] * LANES
    out_ref[:, 0:before] = early_ref[0:rows]
    out_ref[:, inner : inner + before] = early_ref[rows : 2 * rows]
    base = 2 * inner + 2 * groups_width
    out_ref[:, base : base + LANES] = tail_ref[...]

    def store_at(first, second):
        def store(start, width, product):
            out_ref[:, first + start : first + start + width] = product[0:rows]
            out_ref[:, second + start : second + start + width] = product[rows : 2 * rows]

        return store

    multiply_tiles(lhs_ref[...], tiles_ref, store_at(before, inner + before))
    multiply_tiles(lhs_ref[...], tiles_bc_ref, store_at(2 * inner, 2 * inner + groups_width))


def in_proj(tokens, gains, weight_xz, weight_bc, weight_dt):
    rows, depth = tokens.shape
    inner = weight_xz.shape[2]
    groups_width = weight_bc.shape[2]
    heads = weight_dt.shape[1]
    tiles, tiles_bc = inner // LANES, groups_width // LANES
    half = tiles // 2
    xz = weight_xz.reshape(depth, 2, tiles, LANES).transpose(0, 2, 1, 3)
    bc = weight_bc.reshape(depth, 2, tiles_bc, LANES).transpose(0, 2, 1, 3)
    width = 2 * inner + 2 * groups_width + LANES

    def flat(piece):
        return in_vmem(piece.reshape(piece.shape[0], 2 * depth, LANES))

    def piece_of(count):
        return pltpu.VMEM((count, depth, 2, LANES), BF16)

    lhs, tail, piece = call(
        in_load_kernel,
        [shape_of((2 * rows, 2 * depth), BF16), shape_of((rows, LANES), BF16), piece_of(half)],
        [ANY] * 4,
        [in_hbm(one) for one in (tokens, gains, weight_dt.T, xz)],
        6 * MIB,
        "in_load",
        scratch=[
            pltpu.VMEM((rows, depth), BF16),
            pltpu.VMEM(gains.shape, F32),
            pltpu.VMEM((LANES, depth), BF16),
            pltpu.SemaphoreType.DMA((3,)),
            pltpu.SemaphoreType.DMA((half,)),
        ],
        cost=moved(weight_xz.size),
    )
    early, piece, piece_bc = call(
        in_middle_kernel,
        [shape_of((2 * rows, half * LANES), BF16), piece_of(tiles - half), piece_of(tiles_bc)],
        [VM, VM, ANY, ANY],
        (lhs, flat(piece), in_hbm(xz), in_hbm(bc)),
        8 * MIB,
        "in_middle",
        scratch=[pltpu.SemaphoreType.DMA((tiles - half,)), pltpu.SemaphoreType.DMA((tiles_bc,))],
    )
    return call(
        in_last_kernel,
        shape_of((rows, width), BF16),
        [VM] * 5,
        (lhs, early, tail, flat(piece), flat(piece_bc)),
        8 * MIB,
        "in_last",
    )


def moved(size):
    return pl.CostEstimate(flops=0, bytes_accessed=2 * size, transcendentals=0)


def prefetch_kernel(from_ref, to_ref, sem):
    copy = pltpu.make_async_copy(from_ref, to_ref, sem)
    copy.start()
    copy.wait()


def prefetch(weight, after):
    weight, _ = lax.optimization_barrier((weight, after))
    return call(
        prefetch_kernel,
        pltpu.VMEM(weight.shape, BF16),
        [ANY],
        (in_hbm(weight),),
        MIB,
        "prefetch",
        scratch=[pltpu.SemaphoreType.DMA],
        cost=moved(2 * weight.size),
    )


def pick_rows_kernel(local_rows, capacity, slots, ids_ref, own_ref, other_ref, parents_ref, *out_refs):
    code_row, _ = codes(parents_ref, local_rows, capacity, slots)
    total = (own_ref[...].astype(F32) + other_ref[...].astype(F32)).astype(BF16)
    rows = total.shape[0]
    slot = iota((slots, rows), 0)
    for i, out_ref in enumerate(out_refs):
        pick = one_hot(code_row == ids_ref[i] * slots + slot)
        out_ref[...] = dot(pick, total).astype(BF16)


def pick_rows(targets, own, other, parents, local_rows, capacity, slots):
    width = own.shape[1]
    count = targets.shape[0]
    return call(
        functools.partial(pick_rows_kernel, local_rows, capacity, slots),
        [shape_of((slots, width), BF16)] * count,
        [SM, VM, VM, VM],
        (targets, own, other, parents),
        8 * MIB,
        "pick_rows",
    )


def chip_sum_kernel(own_ref, other_ref, out_ref):
    out_ref[...] = (own_ref[...].astype(F32) + other_ref[...].astype(F32)).astype(BF16)


def chip_sum(own, other):
    return call(chip_sum_kernel, shape_of(own.shape, BF16), [VM, VM], (own, other), 4 * MIB, "chip_sum")


def mixer_kernel(parts, heads, capacity, ids_ref, parents_ref, *refs):
    part_refs = refs[:parts]
    (
        conv_ref,
        conv_bc_ref,
        bias_ref,
        rates_ref,
        skip_ref,
        gain_ref,
        queue_ref,
        queue_bc_ref,
        state_hbm,
        act_ref,
        message_ref,
        state_ref,
        sem,
    ) = refs[parts:]
    fetched = [pltpu.make_async_copy(state_hbm.at[r], state_ref.at[r], sem.at[r]) for r in range(state_ref.shape[0])]
    for one in fetched:
        one.start()
    slots = part_refs[0].shape[0]
    inner = gain_ref.shape[1]
    lags, local_rows, _ = queue_ref.shape
    groups_width = queue_bc_ref.shape[3]
    state_size = state_ref.shape[3]
    head_size = state_ref.shape[2]
    groups_here = groups_width // state_size
    per_group = inner // groups_here
    proj = part_refs[0][...].astype(F32)
    for ref in part_refs[1:]:
        proj = proj + ref[...].astype(F32)
    base_bc = 2 * inner
    base = base_bc + 2 * groups_width
    tail = proj[:, base : base + LANES]
    lane = iota(tail.shape, 1)
    squares = jnp.sum(jnp.where((lane == heads) | (lane == heads + 1), tail, 0.0), axis=1, keepdims=True)
    scale = lax.rsqrt(squares / D + EPS)
    code_row, _ = codes(parents_ref, local_rows, capacity, slots)
    slot = iota((slots, code_row.shape[1]), 0)
    mine = code_row == ids_ref[0] * slots + slot
    valid = jnp.sum(jnp.where(mine, 1.0, 0.0), axis=1, keepdims=True)
    parent = jnp.sum(jnp.where(mine, lax.rem(parents_ref[...], local_rows), 0), axis=1, keepdims=True)
    pick = jnp.where((iota((slots, local_rows), 1) == parent) & (valid > 0.0), 1.0, 0.0).astype(BF16)

    now = proj[:, 0:inner] * scale
    gate = proj[:, inner : 2 * inner] * scale
    conv = now * conv_ref[lags : lags + 1, :]
    for k in range(lags):
        held = dot(pick, queue_ref[k])
        conv = conv + held * conv_ref[k : k + 1, :]
        if k > 0:
            message_ref[:, (k - 1) * inner : k * inner] = held.astype(BF16)
    message_ref[:, (lags - 1) * inner : lags * inner] = now.astype(BF16)
    inner_vals = conv * jax.nn.sigmoid(conv)
    at = lags * inner
    keys = []
    for j in range(2):
        start = base_bc + j * groups_width
        now_bc = proj[:, start : start + groups_width] * scale
        conv_bc = now_bc * conv_bc_ref[lags, j : j + 1, :]
        for k in range(lags):
            held = dot(pick, queue_bc_ref[k, j])
            conv_bc = conv_bc + held * conv_bc_ref[k, j : j + 1, :]
            if k > 0:
                to = at + ((k - 1) * 2 + j) * groups_width
                message_ref[:, to : to + groups_width] = held.astype(BF16)
        to = at + ((lags - 1) * 2 + j) * groups_width
        message_ref[:, to : to + groups_width] = now_bc.astype(BF16)
        keys.append(conv_bc * jax.nn.sigmoid(conv_bc))
    at = at + lags * 2 * groups_width

    raw = tail * scale + bias_ref[...]
    steps = jnp.maximum(raw, 0.0) + jnp.log1p(jnp.exp(-jnp.abs(raw)))
    decays = jnp.exp(-steps * rates_ref[...])
    spread = one_hot(iota((LANES, inner), 0) == iota((LANES, inner), 1) // head_size)

    def expand(value):
        high, low = split_two(value)
        return dot(high, spread) + dot(low, spread)

    steps_wide = expand(steps)
    decays_wide = expand(decays)
    skip_wide = expand(jnp.broadcast_to(skip_ref[...], (8, LANES)))[0:1]
    update = steps_wide * inner_vals
    message_ref[:, at : at + inner] = update.astype(BF16)
    at = at + inner
    message_ref[:, at : at + groups_width] = keys[0].astype(BF16)
    at = at + groups_width
    decay_high, decay_low = split_two(decays)
    message_ref[:, at : at + LANES] = decay_high
    message_ref[:, at + LANES : at + 2 * LANES] = decay_low

    for g in range(groups_here):
        lanes = slice(g * state_size, (g + 1) * state_size)
        wide = slice(g * per_group, (g + 1) * per_group)
        b_vals, c_vals = keys[0][:, lanes], keys[1][:, lanes]
        high, low = split_two(c_vals)
        c_both = jnp.concatenate([high, low], axis=0)
        mixed = jnp.zeros((slots, per_group), F32)
        first_head = g * (per_group // head_size)
        for r in range(local_rows):
            if g == 0:
                fetched[r].wait()
            block = state_ref[r, first_head : first_head + per_group // head_size]
            both = dot_t(c_both, block.reshape(per_group, state_size))
            mixed = mixed + jnp.where(parent == r, both[0:slots] + both[slots : 2 * slots], 0.0)
        inside = jnp.sum(b_vals * c_vals, axis=1, keepdims=True)
        mixed = decays_wide[:, wide] * mixed + update[:, wide] * inside + skip_wide[:, wide] * inner_vals[:, wide]
        gated = mixed * (gate[:, wide] * jax.nn.sigmoid(gate[:, wide]))
        mean = jnp.sum(gated * gated, axis=1, keepdims=True) / per_group
        out = gated * lax.rsqrt(mean + EPS) * gain_ref[:, wide]
        act_ref[:, wide] = jnp.where(valid > 0.0, out, 0.0).astype(BF16)


def mixer(ids, parents, capacity, parts, params, queue, queue_bc, state):
    conv, conv_bc, bias, rates, skip, gain = params
    slots = parts[0].shape[0]
    inner = gain.shape[0]
    lags = queue.shape[0]
    groups_width = queue_bc.shape[3]
    heads = bias.shape[0]
    message = lags * (inner + 2 * groups_width) + inner + groups_width + 2 * LANES

    def lane_row(vector):
        return jnp.pad(vector, (0, LANES - heads)).reshape(1, LANES)

    return call(
        functools.partial(mixer_kernel, len(parts), heads, capacity),
        [shape_of((slots, inner), BF16), shape_of((slots, message), BF16)],
        [SM, VM] + [VM] * len(parts) + [VM] * 8 + [ANY],
        (ids, parents, *parts, conv, conv_bc, lane_row(bias), lane_row(rates), lane_row(skip), gain.reshape(1, inner), queue, queue_bc, in_hbm(state)),
        10 * MIB,
        "mixer",
        scratch=[pltpu.VMEM(state.shape, BF16), pltpu.SemaphoreType.DMA((state.shape[0],))],
    )


def deal_kernel(capacity, ids_ref, message_ref, *out_refs):
    slots = message_ref.shape[0]
    count = len(out_refs)
    row = iota((slots, slots), 0)
    want = row
    for i in range(slots // capacity):
        want = jnp.where(row // capacity == i, ids_ref[i] * capacity + row % capacity, want)
    order = one_hot(iota((slots, slots), 1) == want)
    dealt = dot(order, message_ref[...])
    at = 0
    for out_ref in out_refs:
        size = out_ref.shape[0]
        out_ref[...] = dealt[at : at + size].astype(BF16)
        at += size


def deal(targets, message, capacity):
    sizes = [capacity, capacity] + [2 * capacity] * (targets.shape[0] // 2 - 1)
    return call(
        functools.partial(deal_kernel, capacity),
        [shape_of((size, message.shape[1]), BF16) for size in sizes],
        [SM, VM],
        (targets, message),
        8 * MIB,
        "deal",
    )


def collect_kernel(rows, capacity, slots, lags, groups_width, ids_ref, parents_ref, *refs):
    in_refs, (inner_ref, groups_ref, update_ref, keys_ref, decay_ref) = refs[:-5], refs[-5:]
    count = len(in_refs)
    code_row, code_col = codes(parents_ref, rows, capacity, slots)
    everyone = code_col.shape[0]
    inner = update_ref.shape[1]
    me = ids_ref[0]
    parts = []
    for i, ref in enumerate(in_refs):
        value = ref[...].astype(F32)
        start = capacity if i > 1 and i % 2 else 0
        parts.append(value[start : start + capacity])
    held = jnp.concatenate(parts, axis=0).astype(BF16)
    col = iota((everyone, count * capacity), 1)
    want = jnp.full(col.shape, -1, jnp.int32)
    for i in range(count):
        want = jnp.where(col // capacity == i, ids_ref[i] * slots + me * capacity + col % capacity, want)
    chosen = one_hot(code_col == want)
    here = one_hot(iota((rows, everyone), 1) == me * rows + iota((rows, everyone), 0))
    mine = dot(dot(here, chosen).astype(BF16), held)
    for k in range(lags):
        inner_ref[k] = mine[:, k * inner : (k + 1) * inner].astype(BF16)
    at = lags * inner
    for k in range(lags):
        for j in range(2):
            start = at + (2 * k + j) * groups_width
            groups_ref[:, k, j, :] = mine[:, start : start + groups_width].astype(BF16)
    at = at + 2 * lags * groups_width
    update_ref[...] = mine[:, at : at + inner]
    at = at + inner
    keys_ref[...] = mine[:, at : at + groups_width]
    at = at + groups_width
    decay_ref[...] = mine[:, at : at + LANES] + mine[:, at + LANES : at + 2 * LANES]


def collect(sources, parents, rows, messages, slots, inner, groups_width, lags):
    capacity = messages[0].shape[0]
    return call(
        functools.partial(collect_kernel, rows, capacity, slots, lags, groups_width),
        [
            shape_of((lags, rows, inner), BF16),
            shape_of((rows, lags, 2, groups_width), BF16),
            shape_of((rows, inner), F32),
            shape_of((rows, groups_width), F32),
            shape_of((rows, LANES), F32),
        ],
        [SM, VM] + [VM] * len(messages),
        (sources, parents, *messages),
        8 * MIB,
        "collect",
    )


def fetch_row(entry, local_rows, kinds, refs, to, sem):
    kind = entry // local_rows
    row = lax.rem(entry, local_rows)
    for known, ref in zip(kinds, refs):

        @pl.when(kind == known)
        def _(ref=ref):
            pltpu.make_async_copy(ref.at[pl.ds(row, 1)], to, sem).start()


def gather_kernel(local_rows, kinds, table_ref, *refs):
    count = len(kinds)
    in_refs, out_refs, sem = refs[:count], refs[count:-1], refs[-1]
    places = [(ref, i) for ref in out_refs for i in range(ref.shape[0])]
    for j, (ref, i) in enumerate(places):
        fetch_row(table_ref[j], local_rows, kinds, in_refs, ref.at[pl.ds(i, 1)], sem.at[j])
    for j, (ref, i) in enumerate(places):
        pltpu.make_async_copy(in_refs[0].at[pl.ds(0, 1)], ref.at[pl.ds(i, 1)], sem.at[j]).wait()


def gather_rows(table, states, sizes):
    shape = states[0].shape
    return call(
        functools.partial(gather_kernel, shape[0], tuple(range(len(states)))),
        [pltpu.VMEM((size, *shape[1:]), BF16) for size in sizes],
        [SM] + [ANY] * len(states),
        (table, in_hbm(states[0]), *states[1:]),
        MIB,
        "gather_rows",
        scratch=[pltpu.SemaphoreType.DMA((sum(sizes),))],
    )


def update_kernel(kinds, is_mine, table_ref, *refs):
    sources = len(kinds)
    state_refs = refs[:sources]
    update_ref, keys_ref, decay_ref = refs[sources : sources + 3]
    out_ref, held, made, sem_in, sem_out = refs[-5:]
    rows, heads, head_size, state_size = held.shape
    inner = update_ref.shape[1]
    groups_here = keys_ref.shape[1] // state_size
    per_group = inner // groups_here
    heads_group = heads // groups_here

    mine = [is_mine(table_ref[j] // rows) for j in range(rows)]
    for j in range(rows):

        @pl.when(mine[j])
        def _(j=j):
            fetch_row(table_ref[j], rows, kinds, state_refs, held.at[pl.ds(j, 1)], sem_in.at[j])

    spread = one_hot(iota((LANES, inner), 0) == iota((LANES, inner), 1) // head_size)
    high, low = split_two(decay_ref[...])
    decay_high, decay_low = dot(high, spread), dot(low, spread)
    columns = []
    for g in range(groups_here):
        wide = slice(g * per_group, (g + 1) * per_group)
        stacked = jnp.concatenate([update_ref[:, wide], decay_high[:, wide], decay_low[:, wide]], axis=0)
        columns.append(jnp.transpose(stacked).astype(BF16))
    row_id = iota((3 * rows, state_size), 0)
    def renew(j):
        pltpu.make_async_copy(state_refs[0].at[pl.ds(0, 1)], held.at[pl.ds(j, 1)], sem_in.at[j]).wait()
        for g in range(groups_here):
            keys = keys_ref[j : j + 1, g * state_size : (g + 1) * state_size]
            right_keys = jnp.where(row_id == j, keys, 0.0)
            right_ones = jnp.where((row_id == rows + j) | (row_id == 2 * rows + j), 1.0, 0.0)
            right = jnp.concatenate([right_keys, right_ones], axis=1).astype(BF16)
            both = dot(columns[g], right)
            which = slice(g * heads_group, (g + 1) * heads_group)
            before = held[j, which].reshape(per_group, state_size).astype(F32)
            after = both[:, state_size:] * before + both[:, :state_size]
            made[j, which] = after.astype(BF16).reshape(heads_group, head_size, state_size)
        pltpu.make_async_copy(made.at[j], out_ref.at[j], sem_out.at[j]).start()

    for j in range(rows):
        pl.when(mine[j])(functools.partial(renew, j))
    for j in range(rows):

        @pl.when(mine[j])
        def _(j=j):
            pltpu.make_async_copy(made.at[j], out_ref.at[j], sem_out.at[j]).wait()


def update_state(table, states, update, keys, decay, is_mine, before=None):
    kinds = tuple(sorted(states))
    shape = states[0].shape
    args = [table, in_hbm(states[0]), *[states[kind] for kind in kinds[1:]], update, keys, decay]
    specs = [SM] + [ANY] * len(kinds) + [VM] * 3
    aliases = {}
    if before is not None:
        aliases = {len(args): 0}
        args.append(in_hbm(before))
        specs.append(pl.BlockSpec(memory_space=pltpu.HBM))
    return pl.pallas_call(
        functools.partial(update_kernel, kinds, is_mine),
        out_shape=pltpu.HBM(shape, BF16),
        in_specs=specs,
        out_specs=pl.BlockSpec(memory_space=pltpu.HBM),
        scratch_shapes=[
            pltpu.VMEM(shape, BF16),
            pltpu.VMEM(shape, BF16),
            pltpu.SemaphoreType.DMA((shape[0],)),
            pltpu.SemaphoreType.DMA((shape[0],)),
        ],
        input_output_aliases=aliases,
        name="update_state",
        compiler_params=pltpu.CompilerParams(vmem_limit_bytes=16 * MIB),
    )(*args)


def no_rows_kernel(*refs):
    pass


def no_rows(shape, count):
    return pl.pallas_call(
        no_rows_kernel,
        out_shape=[pltpu.HBM(shape, BF16)] * count,
        out_specs=[pl.BlockSpec(memory_space=pltpu.HBM)] * count,
        name="no_rows",
    )()


def fetch_pieces(from_ref, to_ref, sem):
    count = sem.shape[0]
    depth = to_ref.shape[0] // count
    pieces = []
    for i in range(count):
        piece = pl.ds(i * depth, depth)
        copy = pltpu.make_async_copy(from_ref.at[piece], to_ref.at[piece], sem.at[i])
        copy.start()
        pieces.append((slice(i * depth, (i + 1) * depth), copy))
    return pieces


def multiply_pieces(left, weight_ref, pieces):
    total = None
    for piece, copy in pieces:
        copy.wait()
        product = dot(left[:, piece], weight_ref[piece, :])
        total = product if total is None else total + product
    return total


def out_proj_kernel(local_rows, capacity, slots, ids_ref, parents_ref, *refs):
    act_refs, (weight_hbm, out_ref, weight_ref, sem) = refs[:-4], refs[-4:]
    pieces = fetch_pieces(weight_hbm, weight_ref, sem)
    _, code_col = codes(parents_ref, local_rows, capacity, slots)
    rows = code_col.shape[0]
    devices = len(act_refs)
    col = iota((rows, devices * slots), 1)
    want = jnp.full(col.shape, -1, jnp.int32)
    for i in range(devices):
        want = jnp.where(col // slots == i, ids_ref[i] * slots + col % slots, want)
    held = jnp.concatenate([ref[...] for ref in act_refs], axis=0)
    activity = dot(one_hot(code_col == want), held).astype(BF16)
    out_ref[...] = multiply_pieces(activity, weight_ref, pieces).astype(BF16)


def out_proj(sources, parents, local_rows, capacity, acts, weight):
    rows = parents.shape[1]
    return call(
        functools.partial(out_proj_kernel, local_rows, capacity, acts[0].shape[0]),
        shape_of((rows, weight.shape[1]), BF16),
        [SM, VM] + [VM] * len(acts) + [ANY],
        (sources, parents, *acts, in_hbm(weight)),
        12 * MIB,
        "out_proj",
        scratch=[pltpu.VMEM(weight.shape, BF16), pltpu.SemaphoreType.DMA((4,))],
    )


def up_kernel(parts, tok_ref, gain_ref, *refs):
    part_refs = refs[:parts]
    weight_ref, residual_ref, out_ref = refs[parts:]
    residual = tok_ref[...].astype(F32)
    total = part_refs[0][...].astype(F32)
    for ref in part_refs[1:]:
        total = total + ref[...].astype(F32)
    residual = residual + total
    residual_ref[...] = residual
    squares = jnp.sum(residual * residual, axis=1, keepdims=True)
    scaled = (residual * gain_ref[1:2, :]).astype(BF16)
    width = weight_ref.shape[1]
    high, low = split_two(squares)
    lane = iota((scaled.shape[0], LANES), 1)
    out_ref[:, width : width + LANES] = jnp.where(
        lane == 0, high.astype(F32), jnp.where(lane == 1, low.astype(F32), 0.0)
    ).astype(BF16)
    out_ref[:, 0:width] = dot(scaled, weight_ref[...]).astype(BF16)


def up_proj(tokens, gains, parts, weight):
    rows, width = tokens.shape
    return call(
        functools.partial(up_kernel, len(parts)),
        [shape_of((rows, width), F32), shape_of((rows, weight.shape[1] + LANES), BF16)],
        [VM] * (len(parts) + 3),
        (tokens, gains, *parts, in_vmem(weight)),
        8 * MIB,
        "up_proj",
    )


def down_kernel(*refs):
    part_refs, (weight_hbm, out_ref, weight_ref, sem) = refs[:-4], refs[-4:]
    pieces = fetch_pieces(weight_hbm, weight_ref, sem)
    total = part_refs[0][...].astype(F32)
    for ref in part_refs[1:]:
        total = total + ref[...].astype(F32)
    width = weight_ref.shape[0]
    squares = jnp.sum(total[:, width : width + LANES], axis=1, keepdims=True)
    hidden = jnp.maximum(total[:, 0:width] * lax.rsqrt(squares / D + EPS), 0.0)
    out_ref[...] = multiply_pieces((hidden * hidden).astype(BF16), weight_ref, pieces).astype(BF16)


def down_proj(parts, weight):
    rows = parts[0].shape[0]
    return call(
        down_kernel,
        shape_of((rows, weight.shape[1]), BF16),
        [VM] * len(parts) + [ANY],
        (*parts, in_hbm(weight)),
        20 * MIB,
        "down_proj",
        scratch=[pltpu.VMEM(weight.shape, BF16), pltpu.SemaphoreType.DMA((8,))],
    )


def finish_kernel(residual_ref, *refs):
    part_refs, out_ref = refs[:-1], refs[-1]
    total = part_refs[0][...].astype(F32)
    for ref in part_refs[1:]:
        total = total + ref[...].astype(F32)
    out_ref[0] = (residual_ref[...] + total).astype(BF16)


def finish(residual, parts):
    return call(
        finish_kernel,
        shape_of((1, *residual.shape), BF16),
        [VM] * (len(parts) + 1),
        (residual, *parts),
        6 * MIB,
        "finish",
    )


def plan_rows(chosen, chips, local_rows):
    rows = chosen.shape[0]
    both = 2 * local_rows
    same = chosen[:, None] == jnp.arange(rows, dtype=jnp.int32)[None, :]
    needed = jnp.any(same.reshape(chips, both, rows), axis=1).reshape(chips, chips, 2, local_rows)
    small = jnp.arange(local_rows, dtype=jnp.int32)
    before = jnp.sum(jnp.where(small[None, :] < small[:, None], needed[:, :, :, None, :], False), axis=4)
    first = (needed & (before == 0)).reshape(chips, chips, both)
    needed = needed.reshape(chips, chips, both)
    rest = needed & ~first
    wide = jnp.arange(both, dtype=jnp.int32)
    rank = jnp.sum(jnp.where(wide[None, :] < wide[:, None], rest[:, :, None, :], False), axis=3)
    lane = jnp.where(first, wide // local_rows, rank % 2)
    turn = jnp.where(first, 0, 1 + rank // 2)
    return needed, lane.astype(jnp.int32), turn.astype(jnp.int32)


def rounds_of(chosen, chips, local_rows):
    rows = chosen.shape[0]
    same = chosen[:, None] == jnp.arange(rows, dtype=jnp.int32)[None, :]
    needed = jnp.any(same.reshape(chips, 2 * local_rows, rows), axis=1).reshape(chips, chips, 2, local_rows)
    counts = jnp.sum(needed, axis=3).astype(jnp.int32)
    rest = jnp.sum(counts - jnp.minimum(counts, 1), axis=2)
    apart = jnp.arange(chips)[:, None] != jnp.arange(chips)[None, :]
    return jnp.max(jnp.where(apart, 1 + (rest + 1) // 2, 0))


def on_device(
    tokens,
    parents,
    norm_gains,
    weight_xz,
    weight_bc,
    weight_dt,
    conv_inner,
    conv_groups,
    dt_bias,
    rates,
    skip_gain,
    gate_gain,
    weight_out,
    weight_up,
    weight_down,
    ssm_state,
    queue_inner,
    queue_groups,
):
    devices = lax.axis_size("dp")
    chips = devices // 2
    ranks = lax.axis_size("tensor")
    me = lax.axis_index("dp")
    chip, core = me // 2, me % 2
    local_rows = ssm_state.shape[0]
    lags = queue_inner.shape[1]
    inner = queue_inner.shape[2]
    groups_width = queue_groups.shape[3]
    capacity = max(2, 2 * local_rows // devices)
    slots = devices * capacity
    rows = parents.shape[1]
    barrier = lax.optimization_barrier

    def to_dp(value, hop, flip):
        pairs = [(i, ((i // 2 + hop) % chips) * 2 + ((i % 2) ^ flip)) for i in range(devices)]
        return lax.ppermute(value, "dp", pairs)

    def over_tensor(value):
        return [value] + [
            lax.ppermute(value, "tensor", [(i, (i + s) % ranks) for i in range(ranks)]) for s in range(1, ranks)
        ]

    hops = [(hop, flip) for hop in range(chips) for flip in range(2)]
    sources = jnp.stack([((chip + chips - hop) % chips) * 2 + (core ^ flip) for hop, flip in hops]).astype(jnp.int32)
    targets = jnp.stack([((chip + hop) % chips) * 2 + (core ^ flip) for hop, flip in hops]).astype(jnp.int32)

    chosen = parents[0]
    place = jnp.arange(rows, dtype=jnp.int32)

    def after(value, *earlier):
        return barrier((value, *earlier))[0]

    sibling_state = to_dp(ssm_state, 0, 1)
    states = {0: ssm_state, 1: sibling_state}
    first_sent = first_rows(targets, parents, ssm_state)
    first = [to_dp(buffer, hop, 0) for hop, buffer in enumerate(first_sent, 1)]
    partial = in_proj(after(tokens[0], *first_sent), norm_gains, weight_xz, weight_bc, weight_dt)

    near = to_dp(partial, 0, 1)
    most = min(2 * local_rows, 4 * capacity)
    turns = 1 + (max(min(most, local_rows) - 1, most - 2) + 1) // 2
    early = (turns + 1) // 2
    near, *first = barrier((near, *first))
    picked = pick_rows(targets[0::2], partial, near, parents, local_rows, capacity, slots)
    needed, lane, turn = plan_rows(after(chosen, picked[0]), chips, local_rows)
    chip_rows = jnp.arange(2 * local_rows, dtype=jnp.int32)
    entries = ((chip_rows // local_rows) ^ core) * local_rows + chip_rows % local_rows
    send_tables = []
    for hop in range(1, chips):
        to = (chip + hop) % chips
        mine = needed[to, chip] & (lane[to, chip] == core)
        at_turn = mine[None, :] & (turn[to, chip][None, :] == jnp.arange(turns, dtype=jnp.int32)[:, None])
        send_tables.append(jnp.sum(jnp.where(at_turn, entries[None, :], 0), axis=1).astype(jnp.int32))

    def where_from():
        own_chosen = lax.dynamic_slice_in_dim(chosen, me * local_rows, local_rows, 0)
        parent_chip = own_chosen // (2 * local_rows)
        lookup = own_chosen[:, None] == place[None, :]
        lane_of = jnp.sum(jnp.where(lookup, lane[chip].reshape(1, rows), 0), axis=1)
        turn_of = jnp.sum(jnp.where(lookup, turn[chip].reshape(1, rows), 0), axis=1)
        hop_of = (chip + chips - parent_chip) % chips
        here = ((own_chosen // local_rows) % 2) ^ core
        start_of = jnp.minimum(turn_of, early)
        there = 2 + ((hop_of - 1) * 2 + (lane_of ^ core)) * turns + start_of
        inside = jnp.where(parent_chip == chip, own_chosen % local_rows, turn_of - start_of)
        return (jnp.where(parent_chip == chip, here, there) * local_rows + inside).astype(jnp.int32)

    def kind_of(hop, at):
        return 2 + (hop - 1) * 2 * turns + at

    parts = [picked[0]] + [to_dp(picked[hop], hop, 0) for hop in range(1, chips)]

    waiting = []
    for hop in range(1, chips):
        wanted = after(send_tables[hop - 1][1:early], picked[0])
        waiting.append(gather_rows(wanted, [ssm_state, sibling_state], [1] * (early - 1)))
    table = where_from()
    parts[0] = after(parts[0], table, *[some[0] for some in waiting])
    act, message = mixer(
        sources,
        parents,
        capacity,
        parts,
        (conv_inner, conv_groups, dt_bias, rates, skip_gain, gate_gain),
        queue_inner.transpose(1, 0, 2),
        queue_groups.transpose(1, 2, 0, 3),
        ssm_state,
    )
    acts = [act] + [to_dp(act, hop, flip) for hop, flip in hops[1:]]
    arrived, relayed = {0: first}, {}

    def relay(at, *earlier):
        relayed[at] = [to_dp(after(some, *earlier), 0, 1) for some in arrived[at]]

    relay(0, act)
    acts[0], relayed[0] = barrier((acts[0], relayed[0]))


    def send_turn(at, *earlier):
        return [to_dp(after(some[at - 1], *earlier), hop, 0) for hop, some in enumerate(waiting, 1)]

    out_part = out_proj(sources, parents, local_rows, capacity, acts, weight_out)
    arrived[1] = send_turn(1, *acts)
    out_parts = over_tensor(out_part)
    for at in range(2, early - 1):
        arrived[at] = send_turn(at, out_part)
    weight_up = prefetch(weight_up, out_part)
    dealt = deal(targets, after(message, weight_up), capacity)
    out_parts[0], arrived[1], *dealt = barrier((out_parts[0], arrived[1], *dealt))
    residual, up_part = up_proj(tokens[0], norm_gains, out_parts, weight_up)
    last = early - 1
    between = {at: arrived[at] for at in range(2, last)}
    near_up, between = barrier((to_dp(up_part, 0, 1), between))
    arrived.update(between)
    up_chip = chip_sum(up_part, near_up)
    up_parts = [up_chip] + [to_dp(up_chip, hop, 0) for hop in range(1, chips)]

    for at in range(1, last):
        relay(at, up_chip)
    messages = [dealt[0], to_dp(after(dealt[1], up_chip), 0, 1)]
    up_parts[0], relayed = barrier((up_parts[0], relayed))
    sent = [to_dp(after(dealt[1 + hop], *up_parts), hop, 0) for hop in range(1, chips)]
    down_part = down_proj(up_parts, weight_down)
    down_parts = over_tensor(down_part)
    if last > 1:
        arrived[last] = send_turn(last, down_part)

    for some in sent:
        messages += [some, to_dp(after(some, down_part), 0, 1)]
    final_inner, final_groups, update, keys, decay = collect(
        sources, parents, local_rows, messages, slots, inner, groups_width, lags
    )

    def is_early(kind):
        return (kind < 2) | (lax.rem(kind - 2, turns) < last)

    def is_late(kind):
        return jnp.logical_not(is_early(kind))

    chosen = after(chosen, update)
    groups = lax.axis_size("groups")
    longest = rounds_of(chosen, chips, local_rows)
    for shift in range(1, groups):
        other = lax.ppermute(chosen, "groups", [(i, (i + shift) % groups) for i in range(groups)])
        longest = jnp.maximum(longest, rounds_of(other, chips, local_rows))

    def add_states(turn_range):
        for at in turn_range:
            for hop in range(1, chips):
                states[kind_of(hop, at)] = arrived[at][hop - 1]
                states[kind_of(hop, at) + turns] = relayed[at][hop - 1]

    add_states(range(last))
    final_state = update_state(table, states, update, keys, decay, is_early)
    residual, final_state = barrier((residual, final_state))
    beam_out = finish(residual, down_parts)
    relay(last, beam_out)
    add_states([last])

    more = (turns - early, *ssm_state.shape[1:])

    def fetch_more():
        fetched = []
        for hop in range(1, chips):
            wanted = send_tables[hop - 1][early:]
            (buffer,) = gather_rows(wanted, [ssm_state, sibling_state], [turns - early])
            fetched.append(to_dp(buffer, hop, 0))
            fetched.append(to_dp(fetched[-1], 0, 1))
        return tuple(fetched)

    fetched = lax.cond(longest > early, fetch_more, lambda: tuple(no_rows(more, 2 * (chips - 1))))
    late_states = {0: ssm_state}
    for hop in range(1, chips):
        for lane_kind, buffer in ((kind_of(hop, early), fetched[2 * hop - 2]), (kind_of(hop, early) + turns, fetched[2 * hop - 1])):
            late_states[lane_kind] = buffer
        for lane_kind in (kind_of(hop, last), kind_of(hop, last) + turns):
            late_states[lane_kind] = states[lane_kind]
    final_state = update_state(table, late_states, update, keys, decay, is_late, final_state)
    return (beam_out, final_state, final_inner.transpose(1, 0, 2), final_groups)


def solution(mesh):
    in_specs = (
        P(None, "groups", "dp"),
        P(None, "groups"),
        P(None, "dp"),
        P("dp", None, "tensor"),
        P("dp", None, "tensor"),
        P("dp", "tensor"),
        P(None, "tensor"),
        P(None, None, "tensor"),
        P("tensor"),
        P("tensor"),
        P("tensor"),
        P("tensor"),
        P("tensor", "dp"),
        P("dp", "tensor"),
        P("tensor", "dp"),
        P(("groups", "dp"), "tensor", None, None),
        P(("groups", "dp"), None, "tensor"),
        P(("groups", "dp"), None, None, "tensor"),
    )
    out_specs = (
        P(None, "groups", "dp"),
        P(("groups", "dp"), "tensor", None, None),
        P(("groups", "dp"), None, "tensor"),
        P(("groups", "dp"), None, None, "tensor"),
    )
    return jax.shard_map(
        on_device, mesh=mesh, in_specs=in_specs, out_specs=out_specs, check_vma=False
    )
```

```python
import functools

import jax
import jax.numpy as jnp
from jax import lax
from jax.experimental import pallas as pl
from jax.experimental.pallas import tpu as pltpu
from jax.sharding import PartitionSpec as P

D = 8192
H = 128
G = 8
EPS = 1e-05
LANES = 128
MIB = 1 << 20

F32 = jnp.float32
BF16 = jnp.bfloat16

VM = pl.BlockSpec(memory_space=pltpu.VMEM)
SM = pl.BlockSpec(memory_space=pltpu.SMEM)
ANY = pl.BlockSpec(memory_space=pl.ANY)


def dot(a, b):
    return jnp.dot(a, b, preferred_element_type=F32)


def dot_t(a, b):
    return lax.dot_general(a, b, (((1,), (1,)), ((), ())), preferred_element_type=F32)


def iota(shape, dim):
    return lax.broadcasted_iota(jnp.int32, shape, dim)


def one_hot(condition):
    return jnp.where(condition, 1.0, 0.0).astype(BF16)


def codes(parents_ref, local_rows, capacity, slots):
    rows = parents_ref.shape[1]
    parents = parents_ref[...]
    one, other = iota((rows, rows), 0), iota((rows, rows), 1)
    across = jnp.broadcast_to(parents, (rows, rows))
    down = jnp.sum(jnp.where(one == other, across, 0), axis=1, keepdims=True)
    same = (across // local_rows == down // local_rows) & (one // local_rows == other // local_rows)
    rank_row = jnp.sum(jnp.where(same & (one < other), 1, 0), axis=0, keepdims=True)
    rank_col = jnp.sum(jnp.where(same & (other < one), 1, 0), axis=1, keepdims=True)
    code_row = parents // local_rows * slots + iota((1, rows), 1) // local_rows * capacity + rank_row
    code_col = down // local_rows * slots + iota((rows, 1), 0) // local_rows * capacity + rank_col
    return code_row, code_col


def in_hbm(value):
    return pltpu.with_memory_space_constraint(value, pltpu.HBM)


def in_vmem(value):
    return pltpu.with_memory_space_constraint(value, pltpu.VMEM)


def split_two(value):
    high = value.astype(BF16)
    low = (value - high.astype(F32)).astype(BF16)
    return high, low


def call(kernel, outs, in_specs, args, vmem, name, scratch=(), out_specs=None, cost=None):
    single = not isinstance(outs, (list, tuple))
    if out_specs is None:
        out_specs = VM if single else [VM] * len(outs)
    return pl.pallas_call(
        kernel,
        out_shape=outs,
        in_specs=in_specs,
        out_specs=out_specs,
        scratch_shapes=list(scratch),
        name=name,
        cost_estimate=cost,
        compiler_params=pltpu.CompilerParams(vmem_limit_bytes=vmem),
    )(*args)


def shape_of(shape, dtype):
    return jax.ShapeDtypeStruct(shape, dtype)


def first_rows_kernel(ids_ref, parents_ref, state_ref, *refs):
    out_refs, sem = refs[:-1], refs[-1]
    local_rows = state_ref.shape[0]
    both = 2 * local_rows
    me = ids_ref[0]
    copies = []
    for hop, out_ref in enumerate(out_refs, 1):
        to = ids_ref[2 * hop] // 2
        low = jnp.int32(local_rows)
        for i in range(both):
            parent = parents_ref[0, to * both + i]
            here = parent // local_rows == me
            low = jnp.where(here, jnp.minimum(low, lax.rem(parent, local_rows)), low)
        row = jnp.where(low < local_rows, low, 0)
        copies.append(pltpu.make_async_copy(state_ref.at[pl.ds(row, 1)], out_ref, sem.at[hop - 1]))
        copies[-1].start()
    for copy in copies:
        copy.wait()


def first_rows(targets, parents, state):
    count = targets.shape[0] // 2 - 1
    return call(
        first_rows_kernel,
        [pltpu.VMEM((1, *state.shape[1:]), BF16)] * count,
        [SM, SM, ANY],
        (targets, parents, in_hbm(state)),
        MIB,
        "first_rows",
        scratch=[pltpu.SemaphoreType.DMA((count,))],
    )


def in_load_kernel(
    tok_hbm, gain_hbm, dt_hbm, xz_hbm, lhs_ref, tail_ref, piece_ref, tok_ref, gain_ref, dt_ref, sem_small, sem
):
    rows, depth = tok_ref.shape
    heads = dt_hbm.shape[0]
    small = [
        pltpu.make_async_copy(tok_hbm, tok_ref, sem_small.at[0]),
        pltpu.make_async_copy(gain_hbm, gain_ref, sem_small.at[1]),
        pltpu.make_async_copy(dt_hbm, dt_ref.at[pl.ds(0, heads)], sem_small.at[2]),
    ]
    copies = [pltpu.make_async_copy(xz_hbm.at[:, t], piece_ref.at[t], sem.at[t]) for t in range(piece_ref.shape[0])]
    for one in small + copies:
        one.start()
    dt_ref[heads:, :] = jnp.zeros((LANES - heads, depth), BF16)
    small[0].wait()
    small[1].wait()
    inputs = tok_ref[...].astype(F32)
    squares = jnp.sum(inputs * inputs, axis=1, keepdims=True)
    scaled = (inputs * gain_ref[0:1, :]).astype(BF16)
    row = iota((LANES, 4 * LANES), 0)
    col = iota((LANES, 4 * LANES), 1)
    spread = one_hot((col == 2 * row) | (col == 2 * LANES + 2 * row + 1))
    blocks = depth // LANES
    stacked = jnp.concatenate([scaled[:, i * LANES : (i + 1) * LANES] for i in range(blocks)], axis=0)
    wide = dot(stacked, spread).astype(BF16)
    for i in range(blocks):
        where = slice(i * 2 * LANES, (i + 1) * 2 * LANES)
        block = wide[i * rows : (i + 1) * rows]
        lhs_ref[0:rows, where] = block[:, : 2 * LANES]
        lhs_ref[rows : 2 * rows, where] = block[:, 2 * LANES :]
    small[2].wait()
    tail = dot_t(scaled, dt_ref[...])
    high, low = split_two(squares)
    lane = iota(tail.shape, 1)
    tail = jnp.where(lane == heads, high.astype(F32), jnp.where(lane == heads + 1, low.astype(F32), tail))
    tail_ref[...] = tail.astype(BF16)
    for one in copies:
        one.wait()


def multiply_tiles(lhs, tiles_ref, store):
    count = tiles_ref.shape[0]
    step = 2 if count % 2 == 0 else 1
    for t in range(0, count, step):
        weights = tiles_ref[t] if step == 1 else jnp.concatenate([tiles_ref[t], tiles_ref[t + 1]], axis=1)
        store(t * LANES, step * LANES, dot(lhs, weights).astype(BF16))


def in_middle_kernel(lhs_ref, tiles_ref, xz_hbm, bc_hbm, out_ref, piece_ref, piece_bc_ref, sem, sem_bc):
    done = tiles_ref.shape[0]
    copies = [
        pltpu.make_async_copy(xz_hbm.at[:, done + t], piece_ref.at[t], sem.at[t]) for t in range(piece_ref.shape[0])
    ] + [pltpu.make_async_copy(bc_hbm.at[:, t], piece_bc_ref.at[t], sem_bc.at[t]) for t in range(piece_bc_ref.shape[0])]
    for one in copies:
        one.start()

    def store(start, width, product):
        out_ref[:, start : start + width] = product

    multiply_tiles(lhs_ref[...], tiles_ref, store)
    for one in copies:
        one.wait()


def in_last_kernel(lhs_ref, early_ref, tail_ref, tiles_ref, tiles_bc_ref, out_ref):
    rows = tail_ref.shape[0]
    before = early_ref.shape[1]
    inner = before + tiles_ref.shape[0] * LANES
    groups_width = tiles_bc_ref.shape[0] * LANES
    out_ref[:, 0:before] = early_ref[0:rows]
    out_ref[:, inner : inner + before] = early_ref[rows : 2 * rows]
    base = 2 * inner + 2 * groups_width
    out_ref[:, base : base + LANES] = tail_ref[...]

    def store_at(first, second):
        def store(start, width, product):
            out_ref[:, first + start : first + start + width] = product[0:rows]
            out_ref[:, second + start : second + start + width] = product[rows : 2 * rows]

        return store

    multiply_tiles(lhs_ref[...], tiles_ref, store_at(before, inner + before))
    multiply_tiles(lhs_ref[...], tiles_bc_ref, store_at(2 * inner, 2 * inner + groups_width))


def in_proj(tokens, gains, weight_xz, weight_bc, weight_dt):
    rows, depth = tokens.shape
    inner = weight_xz.shape[2]
    groups_width = weight_bc.shape[2]
    heads = weight_dt.shape[1]
    tiles, tiles_bc = inner // LANES, groups_width // LANES
    half = tiles // 2
    xz = weight_xz.reshape(depth, 2, tiles, LANES).transpose(0, 2, 1, 3)
    bc = weight_bc.reshape(depth, 2, tiles_bc, LANES).transpose(0, 2, 1, 3)
    width = 2 * inner + 2 * groups_width + LANES

    def flat(piece):
        return in_vmem(piece.reshape(piece.shape[0], 2 * depth, LANES))

    def piece_of(count):
        return pltpu.VMEM((count, depth, 2, LANES), BF16)

    lhs, tail, piece = call(
        in_load_kernel,
        [shape_of((2 * rows, 2 * depth), BF16), shape_of((rows, LANES), BF16), piece_of(half)],
        [ANY] * 4,
        [in_hbm(one) for one in (tokens, gains, weight_dt.T, xz)],
        6 * MIB,
        "in_load",
        scratch=[
            pltpu.VMEM((rows, depth), BF16),
            pltpu.VMEM(gains.shape, F32),
            pltpu.VMEM((LANES, depth), BF16),
            pltpu.SemaphoreType.DMA((3,)),
            pltpu.SemaphoreType.DMA((half,)),
        ],
        cost=moved(weight_xz.size),
    )
    early, piece, piece_bc = call(
        in_middle_kernel,
        [shape_of((2 * rows, half * LANES), BF16), piece_of(tiles - half), piece_of(tiles_bc)],
        [VM, VM, ANY, ANY],
        (lhs, flat(piece), in_hbm(xz), in_hbm(bc)),
        8 * MIB,
        "in_middle",
        scratch=[pltpu.SemaphoreType.DMA((tiles - half,)), pltpu.SemaphoreType.DMA((tiles_bc,))],
    )
    return call(
        in_last_kernel,
        shape_of((rows, width), BF16),
        [VM] * 5,
        (lhs, early, tail, flat(piece), flat(piece_bc)),
        8 * MIB,
        "in_last",
    )


def moved(size):
    return pl.CostEstimate(flops=0, bytes_accessed=2 * size, transcendentals=0)


def prefetch_kernel(from_ref, to_ref, sem):
    copy = pltpu.make_async_copy(from_ref, to_ref, sem)
    copy.start()
    copy.wait()


def prefetch(weight, after):
    weight, _ = lax.optimization_barrier((weight, after))
    return call(
        prefetch_kernel,
        pltpu.VMEM(weight.shape, BF16),
        [ANY],
        (in_hbm(weight),),
        MIB,
        "prefetch",
        scratch=[pltpu.SemaphoreType.DMA],
        cost=moved(2 * weight.size),
    )


def pick_rows_kernel(local_rows, capacity, slots, ids_ref, own_ref, other_ref, parents_ref, *out_refs):
    code_row, _ = codes(parents_ref, local_rows, capacity, slots)
    total = (own_ref[...].astype(F32) + other_ref[...].astype(F32)).astype(BF16)
    rows = total.shape[0]
    slot = iota((slots, rows), 0)
    for i, out_ref in enumerate(out_refs):
        pick = one_hot(code_row == ids_ref[i] * slots + slot)
        out_ref[...] = dot(pick, total).astype(BF16)


def pick_rows(targets, own, other, parents, local_rows, capacity, slots):
    width = own.shape[1]
    count = targets.shape[0]
    return call(
        functools.partial(pick_rows_kernel, local_rows, capacity, slots),
        [shape_of((slots, width), BF16)] * count,
        [SM, VM, VM, VM],
        (targets, own, other, parents),
        8 * MIB,
        "pick_rows",
    )


def chip_sum_kernel(own_ref, other_ref, out_ref):
    out_ref[...] = (own_ref[...].astype(F32) + other_ref[...].astype(F32)).astype(BF16)


def chip_sum(own, other):
    return call(chip_sum_kernel, shape_of(own.shape, BF16), [VM, VM], (own, other), 4 * MIB, "chip_sum")


def mixer_kernel(parts, heads, capacity, ids_ref, parents_ref, *refs):
    part_refs = refs[:parts]
    (
        conv_ref,
        conv_bc_ref,
        bias_ref,
        rates_ref,
        skip_ref,
        gain_ref,
        queue_ref,
        queue_bc_ref,
        state_hbm,
        act_ref,
        message_ref,
        state_ref,
        sem,
    ) = refs[parts:]
    fetched = [pltpu.make_async_copy(state_hbm.at[r], state_ref.at[r], sem.at[r]) for r in range(state_ref.shape[0])]
    for one in fetched:
        one.start()
    slots = part_refs[0].shape[0]
    inner = gain_ref.shape[1]
    lags, local_rows, _ = queue_ref.shape
    groups_width = queue_bc_ref.shape[3]
    state_size = state_ref.shape[3]
    head_size = state_ref.shape[2]
    groups_here = groups_width // state_size
    per_group = inner // groups_here
    proj = part_refs[0][...].astype(F32)
    for ref in part_refs[1:]:
        proj = proj + ref[...].astype(F32)
    base_bc = 2 * inner
    base = base_bc + 2 * groups_width
    tail = proj[:, base : base + LANES]
    lane = iota(tail.shape, 1)
    squares = jnp.sum(jnp.where((lane == heads) | (lane == heads + 1), tail, 0.0), axis=1, keepdims=True)
    scale = lax.rsqrt(squares / D + EPS)
    code_row, _ = codes(parents_ref, local_rows, capacity, slots)
    slot = iota((slots, code_row.shape[1]), 0)
    mine = code_row == ids_ref[0] * slots + slot
    valid = jnp.sum(jnp.where(mine, 1.0, 0.0), axis=1, keepdims=True)
    parent = jnp.sum(jnp.where(mine, lax.rem(parents_ref[...], local_rows), 0), axis=1, keepdims=True)
    pick = jnp.where((iota((slots, local_rows), 1) == parent) & (valid > 0.0), 1.0, 0.0).astype(BF16)

    now = proj[:, 0:inner] * scale
    gate = proj[:, inner : 2 * inner] * scale
    conv = now * conv_ref[lags : lags + 1, :]
    for k in range(lags):
        held = dot(pick, queue_ref[k])
        conv = conv + held * conv_ref[k : k + 1, :]
        if k > 0:
            message_ref[:, (k - 1) * inner : k * inner] = held.astype(BF16)
    message_ref[:, (lags - 1) * inner : lags * inner] = now.astype(BF16)
    inner_vals = conv * jax.nn.sigmoid(conv)
    at = lags * inner
    keys = []
    for j in range(2):
        start = base_bc + j * groups_width
        now_bc = proj[:, start : start + groups_width] * scale
        conv_bc = now_bc * conv_bc_ref[lags, j : j + 1, :]
        for k in range(lags):
            held = dot(pick, queue_bc_ref[k, j])
            conv_bc = conv_bc + held * conv_bc_ref[k, j : j + 1, :]
            if k > 0:
                to = at + ((k - 1) * 2 + j) * groups_width
                message_ref[:, to : to + groups_width] = held.astype(BF16)
        to = at + ((lags - 1) * 2 + j) * groups_width
        message_ref[:, to : to + groups_width] = now_bc.astype(BF16)
        keys.append(conv_bc * jax.nn.sigmoid(conv_bc))
    at = at + lags * 2 * groups_width

    raw = tail * scale + bias_ref[...]
    steps = jnp.maximum(raw, 0.0) + jnp.log1p(jnp.exp(-jnp.abs(raw)))
    decays = jnp.exp(-steps * rates_ref[...])
    spread = one_hot(iota((LANES, inner), 0) == iota((LANES, inner), 1) // head_size)

    def expand(value):
        high, low = split_two(value)
        return dot(high, spread) + dot(low, spread)

    steps_wide = expand(steps)
    decays_wide = expand(decays)
    skip_wide = expand(jnp.broadcast_to(skip_ref[...], (8, LANES)))[0:1]
    update = steps_wide * inner_vals
    message_ref[:, at : at + inner] = update.astype(BF16)
    at = at + inner
    message_ref[:, at : at + groups_width] = keys[0].astype(BF16)
    at = at + groups_width
    decay_high, decay_low = split_two(decays)
    message_ref[:, at : at + LANES] = decay_high
    message_ref[:, at + LANES : at + 2 * LANES] = decay_low

    for g in range(groups_here):
        lanes = slice(g * state_size, (g + 1) * state_size)
        wide = slice(g * per_group, (g + 1) * per_group)
        b_vals, c_vals = keys[0][:, lanes], keys[1][:, lanes]
        high, low = split_two(c_vals)
        c_both = jnp.concatenate([high, low], axis=0)
        mixed = jnp.zeros((slots, per_group), F32)
        first_head = g * (per_group // head_size)
        for r in range(local_rows):
            if g == 0:
                fetched[r].wait()
            block = state_ref[r, first_head : first_head + per_group // head_size]
            both = dot_t(c_both, block.reshape(per_group, state_size))
            mixed = mixed + jnp.where(parent == r, both[0:slots] + both[slots : 2 * slots], 0.0)
        inside = jnp.sum(b_vals * c_vals, axis=1, keepdims=True)
        mixed = decays_wide[:, wide] * mixed + update[:, wide] * inside + skip_wide[:, wide] * inner_vals[:, wide]
        gated = mixed * (gate[:, wide] * jax.nn.sigmoid(gate[:, wide]))
        mean = jnp.sum(gated * gated, axis=1, keepdims=True) / per_group
        out = gated * lax.rsqrt(mean + EPS) * gain_ref[:, wide]
        act_ref[:, wide] = jnp.where(valid > 0.0, out, 0.0).astype(BF16)


def mixer(ids, parents, capacity, parts, params, queue, queue_bc, state):
    conv, conv_bc, bias, rates, skip, gain = params
    slots = parts[0].shape[0]
    inner = gain.shape[0]
    lags = queue.shape[0]
    groups_width = queue_bc.shape[3]
    heads = bias.shape[0]
    message = lags * (inner + 2 * groups_width) + inner + groups_width + 2 * LANES

    def lane_row(vector):
        return jnp.pad(vector, (0, LANES - heads)).reshape(1, LANES)

    return call(
        functools.partial(mixer_kernel, len(parts), heads, capacity),
        [shape_of((slots, inner), BF16), shape_of((slots, message), BF16)],
        [SM, VM] + [VM] * len(parts) + [VM] * 8 + [ANY],
        (ids, parents, *parts, conv, conv_bc, lane_row(bias), lane_row(rates), lane_row(skip), gain.reshape(1, inner), queue, queue_bc, in_hbm(state)),
        10 * MIB,
        "mixer",
        scratch=[pltpu.VMEM(state.shape, BF16), pltpu.SemaphoreType.DMA((state.shape[0],))],
    )


def deal_kernel(capacity, ids_ref, message_ref, *out_refs):
    slots = message_ref.shape[0]
    count = len(out_refs)
    row = iota((slots, slots), 0)
    want = row
    for i in range(slots // capacity):
        want = jnp.where(row // capacity == i, ids_ref[i] * capacity + row % capacity, want)
    order = one_hot(iota((slots, slots), 1) == want)
    dealt = dot(order, message_ref[...])
    at = 0
    for out_ref in out_refs:
        size = out_ref.shape[0]
        out_ref[...] = dealt[at : at + size].astype(BF16)
        at += size


def deal(targets, message, capacity):
    sizes = [capacity, capacity] + [2 * capacity] * (targets.shape[0] // 2 - 1)
    return call(
        functools.partial(deal_kernel, capacity),
        [shape_of((size, message.shape[1]), BF16) for size in sizes],
        [SM, VM],
        (targets, message),
        8 * MIB,
        "deal",
    )


def collect_kernel(rows, capacity, slots, lags, groups_width, ids_ref, parents_ref, *refs):
    in_refs, (inner_ref, groups_ref, update_ref, keys_ref, decay_ref) = refs[:-5], refs[-5:]
    count = len(in_refs)
    code_row, code_col = codes(parents_ref, rows, capacity, slots)
    everyone = code_col.shape[0]
    inner = update_ref.shape[1]
    me = ids_ref[0]
    parts = []
    for i, ref in enumerate(in_refs):
        value = ref[...].astype(F32)
        start = capacity if i > 1 and i % 2 else 0
        parts.append(value[start : start + capacity])
    held = jnp.concatenate(parts, axis=0).astype(BF16)
    col = iota((everyone, count * capacity), 1)
    want = jnp.full(col.shape, -1, jnp.int32)
    for i in range(count):
        want = jnp.where(col // capacity == i, ids_ref[i] * slots + me * capacity + col % capacity, want)
    chosen = one_hot(code_col == want)
    here = one_hot(iota((rows, everyone), 1) == me * rows + iota((rows, everyone), 0))
    mine = dot(dot(here, chosen).astype(BF16), held)
    for k in range(lags):
        inner_ref[k] = mine[:, k * inner : (k + 1) * inner].astype(BF16)
    at = lags * inner
    for k in range(lags):
        for j in range(2):
            start = at + (2 * k + j) * groups_width
            groups_ref[:, k, j, :] = mine[:, start : start + groups_width].astype(BF16)
    at = at + 2 * lags * groups_width
    update_ref[...] = mine[:, at : at + inner]
    at = at + inner
    keys_ref[...] = mine[:, at : at + groups_width]
    at = at + groups_width
    decay_ref[...] = mine[:, at : at + LANES] + mine[:, at + LANES : at + 2 * LANES]


def collect(sources, parents, rows, messages, slots, inner, groups_width, lags):
    capacity = messages[0].shape[0]
    return call(
        functools.partial(collect_kernel, rows, capacity, slots, lags, groups_width),
        [
            shape_of((lags, rows, inner), BF16),
            shape_of((rows, lags, 2, groups_width), BF16),
            shape_of((rows, inner), F32),
            shape_of((rows, groups_width), F32),
            shape_of((rows, LANES), F32),
        ],
        [SM, VM] + [VM] * len(messages),
        (sources, parents, *messages),
        8 * MIB,
        "collect",
    )


def fetch_row(entry, local_rows, kinds, refs, to, sem):
    kind = entry // local_rows
    row = lax.rem(entry, local_rows)
    for known, ref in zip(kinds, refs):

        @pl.when(kind == known)
        def _(ref=ref):
            pltpu.make_async_copy(ref.at[pl.ds(row, 1)], to, sem).start()


def gather_kernel(local_rows, kinds, table_ref, *refs):
    count = len(kinds)
    in_refs, out_refs, sem = refs[:count], refs[count:-1], refs[-1]
    places = [(ref, i) for ref in out_refs for i in range(ref.shape[0])]
    for j, (ref, i) in enumerate(places):
        fetch_row(table_ref[j], local_rows, kinds, in_refs, ref.at[pl.ds(i, 1)], sem.at[j])
    for j, (ref, i) in enumerate(places):
        pltpu.make_async_copy(in_refs[0].at[pl.ds(0, 1)], ref.at[pl.ds(i, 1)], sem.at[j]).wait()


def gather_rows(table, states, sizes):
    shape = states[0].shape
    return call(
        functools.partial(gather_kernel, shape[0], tuple(range(len(states)))),
        [pltpu.VMEM((size, *shape[1:]), BF16) for size in sizes],
        [SM] + [ANY] * len(states),
        (table, in_hbm(states[0]), *states[1:]),
        MIB,
        "gather_rows",
        scratch=[pltpu.SemaphoreType.DMA((sum(sizes),))],
    )


def update_kernel(kinds, is_mine, table_ref, *refs):
    sources = len(kinds)
    state_refs = refs[:sources]
    update_ref, keys_ref, decay_ref = refs[sources : sources + 3]
    out_ref, held, made, sem_in, sem_out = refs[-5:]
    rows, heads, head_size, state_size = held.shape
    inner = update_ref.shape[1]
    groups_here = keys_ref.shape[1] // state_size
    per_group = inner // groups_here
    heads_group = heads // groups_here

    mine = [is_mine(table_ref[j] // rows) for j in range(rows)]
    for j in range(rows):

        @pl.when(mine[j])
        def _(j=j):
            fetch_row(table_ref[j], rows, kinds, state_refs, held.at[pl.ds(j, 1)], sem_in.at[j])

    spread = one_hot(iota((LANES, inner), 0) == iota((LANES, inner), 1) // head_size)
    high, low = split_two(decay_ref[...])
    decay_high, decay_low = dot(high, spread), dot(low, spread)
    columns = []
    for g in range(groups_here):
        wide = slice(g * per_group, (g + 1) * per_group)
        stacked = jnp.concatenate([update_ref[:, wide], decay_high[:, wide], decay_low[:, wide]], axis=0)
        columns.append(jnp.transpose(stacked).astype(BF16))
    row_id = iota((3 * rows, state_size), 0)
    def renew(j):
        pltpu.make_async_copy(state_refs[0].at[pl.ds(0, 1)], held.at[pl.ds(j, 1)], sem_in.at[j]).wait()
        for g in range(groups_here):
            keys = keys_ref[j : j + 1, g * state_size : (g + 1) * state_size]
            right_keys = jnp.where(row_id == j, keys, 0.0)
            right_ones = jnp.where((row_id == rows + j) | (row_id == 2 * rows + j), 1.0, 0.0)
            right = jnp.concatenate([right_keys, right_ones], axis=1).astype(BF16)
            both = dot(columns[g], right)
            which = slice(g * heads_group, (g + 1) * heads_group)
            before = held[j, which].reshape(per_group, state_size).astype(F32)
            after = both[:, state_size:] * before + both[:, :state_size]
            made[j, which] = after.astype(BF16).reshape(heads_group, head_size, state_size)
        pltpu.make_async_copy(made.at[j], out_ref.at[j], sem_out.at[j]).start()

    for j in range(rows):
        pl.when(mine[j])(functools.partial(renew, j))
    for j in range(rows):

        @pl.when(mine[j])
        def _(j=j):
            pltpu.make_async_copy(made.at[j], out_ref.at[j], sem_out.at[j]).wait()


def update_state(table, states, update, keys, decay, is_mine, before=None):
    kinds = tuple(sorted(states))
    shape = states[0].shape
    args = [table, in_hbm(states[0]), *[states[kind] for kind in kinds[1:]], update, keys, decay]
    specs = [SM] + [ANY] * len(kinds) + [VM] * 3
    aliases = {}
    if before is not None:
        aliases = {len(args): 0}
        args.append(in_hbm(before))
        specs.append(pl.BlockSpec(memory_space=pltpu.HBM))
    return pl.pallas_call(
        functools.partial(update_kernel, kinds, is_mine),
        out_shape=pltpu.HBM(shape, BF16),
        in_specs=specs,
        out_specs=pl.BlockSpec(memory_space=pltpu.HBM),
        scratch_shapes=[
            pltpu.VMEM(shape, BF16),
            pltpu.VMEM(shape, BF16),
            pltpu.SemaphoreType.DMA((shape[0],)),
            pltpu.SemaphoreType.DMA((shape[0],)),
        ],
        input_output_aliases=aliases,
        name="update_state",
        compiler_params=pltpu.CompilerParams(vmem_limit_bytes=16 * MIB),
    )(*args)


def no_rows_kernel(*refs):
    pass


def no_rows(shape, count):
    return pl.pallas_call(
        no_rows_kernel,
        out_shape=[pltpu.HBM(shape, BF16)] * count,
        out_specs=[pl.BlockSpec(memory_space=pltpu.HBM)] * count,
        name="no_rows",
    )()


def fetch_pieces(from_ref, to_ref, sem):
    count = sem.shape[0]
    depth = to_ref.shape[0] // count
    pieces = []
    for i in range(count):
        piece = pl.ds(i * depth, depth)
        copy = pltpu.make_async_copy(from_ref.at[piece], to_ref.at[piece], sem.at[i])
        copy.start()
        pieces.append((slice(i * depth, (i + 1) * depth), copy))
    return pieces


def multiply_pieces(left, weight_ref, pieces):
    total = None
    for piece, copy in pieces:
        copy.wait()
        product = dot(left[:, piece], weight_ref[piece, :])
        total = product if total is None else total + product
    return total


def out_proj_kernel(local_rows, capacity, slots, ids_ref, parents_ref, *refs):
    act_refs, (weight_hbm, out_ref, weight_ref, sem) = refs[:-4], refs[-4:]
    pieces = fetch_pieces(weight_hbm, weight_ref, sem)
    _, code_col = codes(parents_ref, local_rows, capacity, slots)
    rows = code_col.shape[0]
    devices = len(act_refs)
    col = iota((rows, devices * slots), 1)
    want = jnp.full(col.shape, -1, jnp.int32)
    for i in range(devices):
        want = jnp.where(col // slots == i, ids_ref[i] * slots + col % slots, want)
    held = jnp.concatenate([ref[...] for ref in act_refs], axis=0)
    activity = dot(one_hot(code_col == want), held).astype(BF16)
    out_ref[...] = multiply_pieces(activity, weight_ref, pieces).astype(BF16)


def out_proj(sources, parents, local_rows, capacity, acts, weight):
    rows = parents.shape[1]
    return call(
        functools.partial(out_proj_kernel, local_rows, capacity, acts[0].shape[0]),
        shape_of((rows, weight.shape[1]), BF16),
        [SM, VM] + [VM] * len(acts) + [ANY],
        (sources, parents, *acts, in_hbm(weight)),
        12 * MIB,
        "out_proj",
        scratch=[pltpu.VMEM(weight.shape, BF16), pltpu.SemaphoreType.DMA((4,))],
    )


def up_kernel(parts, tok_ref, gain_ref, *refs):
    part_refs = refs[:parts]
    weight_ref, residual_ref, out_ref = refs[parts:]
    residual = tok_ref[...].astype(F32)
    total = part_refs[0][...].astype(F32)
    for ref in part_refs[1:]:
        total = total + ref[...].astype(F32)
    residual = residual + total
    residual_ref[...] = residual
    squares = jnp.sum(residual * residual, axis=1, keepdims=True)
    scaled = (residual * gain_ref[1:2, :]).astype(BF16)
    width = weight_ref.shape[1]
    high, low = split_two(squares)
    lane = iota((scaled.shape[0], LANES), 1)
    out_ref[:, width : width + LANES] = jnp.where(
        lane == 0, high.astype(F32), jnp.where(lane == 1, low.astype(F32), 0.0)
    ).astype(BF16)
    out_ref[:, 0:width] = dot(scaled, weight_ref[...]).astype(BF16)


def up_proj(tokens, gains, parts, weight):
    rows, width = tokens.shape
    return call(
        functools.partial(up_kernel, len(parts)),
        [shape_of((rows, width), F32), shape_of((rows, weight.shape[1] + LANES), BF16)],
        [VM] * (len(parts) + 3),
        (tokens, gains, *parts, in_vmem(weight)),
        8 * MIB,
        "up_proj",
    )


def down_kernel(*refs):
    part_refs, (weight_hbm, out_ref, weight_ref, sem) = refs[:-4], refs[-4:]
    pieces = fetch_pieces(weight_hbm, weight_ref, sem)
    total = part_refs[0][...].astype(F32)
    for ref in part_refs[1:]:
        total = total + ref[...].astype(F32)
    width = weight_ref.shape[0]
    squares = jnp.sum(total[:, width : width + LANES], axis=1, keepdims=True)
    hidden = jnp.maximum(total[:, 0:width] * lax.rsqrt(squares / D + EPS), 0.0)
    out_ref[...] = multiply_pieces((hidden * hidden).astype(BF16), weight_ref, pieces).astype(BF16)


def down_proj(parts, weight):
    rows = parts[0].shape[0]
    return call(
        down_kernel,
        shape_of((rows, weight.shape[1]), BF16),
        [VM] * len(parts) + [ANY],
        (*parts, in_hbm(weight)),
        20 * MIB,
        "down_proj",
        scratch=[pltpu.VMEM(weight.shape, BF16), pltpu.SemaphoreType.DMA((8,))],
    )


def finish_kernel(residual_ref, *refs):
    part_refs, out_ref = refs[:-1], refs[-1]
    total = part_refs[0][...].astype(F32)
    for ref in part_refs[1:]:
        total = total + ref[...].astype(F32)
    out_ref[0] = (residual_ref[...] + total).astype(BF16)


def finish(residual, parts):
    return call(
        finish_kernel,
        shape_of((1, *residual.shape), BF16),
        [VM] * (len(parts) + 1),
        (residual, *parts),
        6 * MIB,
        "finish",
    )


def plan_rows(chosen, chips, local_rows):
    rows = chosen.shape[0]
    both = 2 * local_rows
    same = chosen[:, None] == jnp.arange(rows, dtype=jnp.int32)[None, :]
    needed = jnp.any(same.reshape(chips, both, rows), axis=1).reshape(chips, chips, 2, local_rows)
    small = jnp.arange(local_rows, dtype=jnp.int32)
    before = jnp.sum(jnp.where(small[None, :] < small[:, None], needed[:, :, :, None, :], False), axis=4)
    first = (needed & (before == 0)).reshape(chips, chips, both)
    needed = needed.reshape(chips, chips, both)
    rest = needed & ~first
    wide = jnp.arange(both, dtype=jnp.int32)
    rank = jnp.sum(jnp.where(wide[None, :] < wide[:, None], rest[:, :, None, :], False), axis=3)
    lane = jnp.where(first, wide // local_rows, rank % 2)
    turn = jnp.where(first, 0, 1 + rank // 2)
    return needed, lane.astype(jnp.int32), turn.astype(jnp.int32)


def rounds_of(chosen, chips, local_rows):
    rows = chosen.shape[0]
    same = chosen[:, None] == jnp.arange(rows, dtype=jnp.int32)[None, :]
    needed = jnp.any(same.reshape(chips, 2 * local_rows, rows), axis=1).reshape(chips, chips, 2, local_rows)
    counts = jnp.sum(needed, axis=3).astype(jnp.int32)
    rest = jnp.sum(counts - jnp.minimum(counts, 1), axis=2)
    apart = jnp.arange(chips)[:, None] != jnp.arange(chips)[None, :]
    return jnp.max(jnp.where(apart, 1 + (rest + 1) // 2, 0))


def on_device(
    tokens,
    parents,
    norm_gains,
    weight_xz,
    weight_bc,
    weight_dt,
    conv_inner,
    conv_groups,
    dt_bias,
    rates,
    skip_gain,
    gate_gain,
    weight_out,
    weight_up,
    weight_down,
    ssm_state,
    queue_inner,
    queue_groups,
):
    devices = lax.axis_size("dp")
    chips = devices // 2
    ranks = lax.axis_size("tensor")
    me = lax.axis_index("dp")
    chip, core = me // 2, me % 2
    local_rows = ssm_state.shape[0]
    lags = queue_inner.shape[1]
    inner = queue_inner.shape[2]
    groups_width = queue_groups.shape[3]
    capacity = max(2, 2 * local_rows // devices)
    slots = devices * capacity
    rows = parents.shape[1]
    barrier = lax.optimization_barrier

    def to_dp(value, hop, flip):
        pairs = [(i, ((i // 2 + hop) % chips) * 2 + ((i % 2) ^ flip)) for i in range(devices)]
        return lax.ppermute(value, "dp", pairs)

    def over_tensor(value):
        return [value] + [
            lax.ppermute(value, "tensor", [(i, (i + s) % ranks) for i in range(ranks)]) for s in range(1, ranks)
        ]

    hops = [(hop, flip) for hop in range(chips) for flip in range(2)]
    sources = jnp.stack([((chip + chips - hop) % chips) * 2 + (core ^ flip) for hop, flip in hops]).astype(jnp.int32)
    targets = jnp.stack([((chip + hop) % chips) * 2 + (core ^ flip) for hop, flip in hops]).astype(jnp.int32)

    chosen = parents[0]
    place = jnp.arange(rows, dtype=jnp.int32)

    def after(value, *earlier):
        return barrier((value, *earlier))[0]

    sibling_state = to_dp(ssm_state, 0, 1)
    states = {0: ssm_state, 1: sibling_state}
    first_sent = first_rows(targets, parents, ssm_state)
    first = [to_dp(buffer, hop, 0) for hop, buffer in enumerate(first_sent, 1)]
    partial = in_proj(after(tokens[0], *first_sent), norm_gains, weight_xz, weight_bc, weight_dt)

    near = to_dp(partial, 0, 1)
    most = min(2 * local_rows, 4 * capacity)
    turns = 1 + (max(min(most, local_rows) - 1, most - 2) + 1) // 2
    early = min(turns, max(3, (turns + 2) // 2))
    single = min(3, early)
    near, *first = barrier((near, *first))
    picked = pick_rows(targets[0::2], partial, near, parents, local_rows, capacity, slots)
    needed, lane, turn = plan_rows(after(chosen, picked[0]), chips, local_rows)
    chip_rows = jnp.arange(2 * local_rows, dtype=jnp.int32)
    entries = ((chip_rows // local_rows) ^ core) * local_rows + chip_rows % local_rows
    send_tables = []
    for hop in range(1, chips):
        to = (chip + hop) % chips
        mine = needed[to, chip] & (lane[to, chip] == core)
        at_turn = mine[None, :] & (turn[to, chip][None, :] == jnp.arange(turns, dtype=jnp.int32)[:, None])
        send_tables.append(jnp.sum(jnp.where(at_turn, entries[None, :], 0), axis=1).astype(jnp.int32))

    def where_from():
        own_chosen = lax.dynamic_slice_in_dim(chosen, me * local_rows, local_rows, 0)
        parent_chip = own_chosen // (2 * local_rows)
        lookup = own_chosen[:, None] == place[None, :]
        lane_of = jnp.sum(jnp.where(lookup, lane[chip].reshape(1, rows), 0), axis=1)
        turn_of = jnp.sum(jnp.where(lookup, turn[chip].reshape(1, rows), 0), axis=1)
        hop_of = (chip + chips - parent_chip) % chips
        here = ((own_chosen // local_rows) % 2) ^ core
        start_of = jnp.where(turn_of >= early, early, jnp.minimum(turn_of, single))
        there = 2 + ((hop_of - 1) * 2 + (lane_of ^ core)) * turns + start_of
        inside = jnp.where(parent_chip == chip, own_chosen % local_rows, turn_of - start_of)
        return (jnp.where(parent_chip == chip, here, there) * local_rows + inside).astype(jnp.int32)

    def kind_of(hop, at):
        return 2 + (hop - 1) * 2 * turns + at

    parts = [picked[0]] + [to_dp(picked[hop], hop, 0) for hop in range(1, chips)]

    waiting = []
    sizes = [1] * (single - 1) + [early - single] * (early > single)
    for hop in range(1, chips):
        wanted = after(send_tables[hop - 1][1:early], picked[0])
        waiting.append(gather_rows(wanted, [ssm_state, sibling_state], sizes))
    table = where_from()
    parts[0] = after(parts[0], table, *[some[0] for some in waiting])
    act, message = mixer(
        sources,
        parents,
        capacity,
        parts,
        (conv_inner, conv_groups, dt_bias, rates, skip_gain, gate_gain),
        queue_inner.transpose(1, 0, 2),
        queue_groups.transpose(1, 2, 0, 3),
        ssm_state,
    )
    acts = [act] + [to_dp(act, hop, flip) for hop, flip in hops[1:]]
    arrived, relayed = {0: first}, {}

    def relay(at, *earlier):
        relayed[at] = [to_dp(after(some, *earlier), 0, 1) for some in arrived[at]]

    relay(0, act)
    acts[0], relayed[0] = barrier((acts[0], relayed[0]))


    def send_turn(at, *earlier):
        return [to_dp(after(some[at - 1], *earlier), hop, 0) for hop, some in enumerate(waiting, 1)]

    out_part = out_proj(sources, parents, local_rows, capacity, acts, weight_out)
    arrived[1] = send_turn(1, *acts)
    out_parts = over_tensor(out_part)
    for at in range(2, single):
        arrived[at] = send_turn(at, out_part)
    weight_up = prefetch(weight_up, out_part)
    dealt = deal(targets, after(message, weight_up), capacity)
    out_parts[0], arrived[1], *dealt = barrier((out_parts[0], arrived[1], *dealt))
    residual, up_part = up_proj(tokens[0], norm_gains, out_parts, weight_up)
    sent = [to_dp(dealt[1 + hop], hop, 0) for hop in range(1, chips)]
    between = {at: arrived[at] for at in range(2, single)}
    near_up, between, sent = barrier((to_dp(up_part, 0, 1), between, sent))
    arrived.update(between)
    up_chip = chip_sum(up_part, near_up)
    up_parts = [up_chip] + [to_dp(up_chip, hop, 0) for hop in range(1, chips)]

    for at in range(1, single):
        relay(at, up_chip)
    messages = [dealt[0], to_dp(after(dealt[1], up_chip), 0, 1)]
    for some in sent:
        messages += [some, to_dp(after(some, up_chip), 0, 1)]
    final_inner, final_groups, update, keys, decay = collect(
        sources, parents, local_rows, messages, slots, inner, groups_width, lags
    )
    up_parts[0], relayed, update = barrier((up_parts[0], relayed, update))
    if early > single:
        arrived[single] = send_turn(single, *up_parts)
    down_part = down_proj(up_parts, weight_down)
    down_parts = over_tensor(down_part)

    def is_early(kind):
        return (kind < 2) | (lax.rem(kind - 2, turns) < single)

    def is_late(kind):
        return jnp.logical_not(is_early(kind))

    def add_states(turn_range):
        for at in turn_range:
            for hop in range(1, chips):
                states[kind_of(hop, at)] = arrived[at][hop - 1]
                states[kind_of(hop, at) + turns] = relayed[at][hop - 1]

    add_states(range(single))
    final_state = update_state(table, states, update, keys, decay, is_early)
    chosen = after(chosen, final_state)
    groups = lax.axis_size("groups")
    longest = rounds_of(chosen, chips, local_rows)
    for shift in range(1, groups):
        other = lax.ppermute(chosen, "groups", [(i, (i + shift) % groups) for i in range(groups)])
        longest = jnp.maximum(longest, rounds_of(other, chips, local_rows))
    residual, final_state, longest = barrier((residual, final_state, longest))
    beam_out = finish(residual, down_parts)
    if early > single:
        relay(single, beam_out)
        add_states([single])

    more = (turns - early, *ssm_state.shape[1:])

    def fetch_more():
        fetched = []
        for hop in range(1, chips):
            wanted = send_tables[hop - 1][early:]
            (buffer,) = gather_rows(wanted, [ssm_state, sibling_state], [turns - early])
            fetched.append(to_dp(buffer, hop, 0))
            fetched.append(to_dp(fetched[-1], 0, 1))
        return tuple(fetched)

    fetched = []
    if turns > early:
        fetched = lax.cond(longest > early, fetch_more, lambda: tuple(no_rows(more, 2 * (chips - 1))))
    late_states = {0: ssm_state}
    for hop in range(1, chips):
        if turns > early:
            late_states[kind_of(hop, early)] = fetched[2 * hop - 2]
            late_states[kind_of(hop, early) + turns] = fetched[2 * hop - 1]
        if early > single:
            for kind in (kind_of(hop, single), kind_of(hop, single) + turns):
                late_states[kind] = states[kind]
    final_state = update_state(table, late_states, update, keys, decay, is_late, final_state)
    return (beam_out, final_state, final_inner.transpose(1, 0, 2), final_groups)


def solution(mesh):
    in_specs = (
        P(None, "groups", "dp"),
        P(None, "groups"),
        P(None, "dp"),
        P("dp", None, "tensor"),
        P("dp", None, "tensor"),
        P("dp", "tensor"),
        P(None, "tensor"),
        P(None, None, "tensor"),
        P("tensor"),
        P("tensor"),
        P("tensor"),
        P("tensor"),
        P("tensor", "dp"),
        P("dp", "tensor"),
        P("tensor", "dp"),
        P(("groups", "dp"), "tensor", None, None),
        P(("groups", "dp"), None, "tensor"),
        P(("groups", "dp"), None, None, "tensor"),
    )
    out_specs = (
        P(None, "groups", "dp"),
        P(("groups", "dp"), "tensor", None, None),
        P(("groups", "dp"), None, "tensor"),
        P(("groups", "dp"), None, None, "tensor"),
    )
    return jax.shard_map(
        on_device, mesh=mesh, in_specs=in_specs, out_specs=out_specs, check_vma=False
    )
```

```python
import functools

import jax
import jax.numpy as jnp
from jax import lax
from jax.experimental import pallas as pl
from jax.experimental.pallas import tpu as pltpu
from jax.sharding import PartitionSpec as P

D = 8192
H = 128
G = 8
EPS = 1e-05
LANES = 128
MIB = 1 << 20

F32 = jnp.float32
BF16 = jnp.bfloat16

VM = pl.BlockSpec(memory_space=pltpu.VMEM)
SM = pl.BlockSpec(memory_space=pltpu.SMEM)
ANY = pl.BlockSpec(memory_space=pl.ANY)


def dot(a, b):
    return jnp.dot(a, b, preferred_element_type=F32)


def dot_t(a, b):
    return lax.dot_general(a, b, (((1,), (1,)), ((), ())), preferred_element_type=F32)


def iota(shape, dim):
    return lax.broadcasted_iota(jnp.int32, shape, dim)


def one_hot(condition):
    return jnp.where(condition, 1.0, 0.0).astype(BF16)


def codes(parents_ref, local_rows, capacity, slots):
    rows = parents_ref.shape[1]
    parents = parents_ref[...]
    one, other = iota((rows, rows), 0), iota((rows, rows), 1)
    across = jnp.broadcast_to(parents, (rows, rows))
    down = jnp.sum(jnp.where(one == other, across, 0), axis=1, keepdims=True)
    same = (across // local_rows == down // local_rows) & (one // local_rows == other // local_rows)
    rank_row = jnp.sum(jnp.where(same & (one < other), 1, 0), axis=0, keepdims=True)
    rank_col = jnp.sum(jnp.where(same & (other < one), 1, 0), axis=1, keepdims=True)
    code_row = parents // local_rows * slots + iota((1, rows), 1) // local_rows * capacity + rank_row
    code_col = down // local_rows * slots + iota((rows, 1), 0) // local_rows * capacity + rank_col
    return code_row, code_col


def in_hbm(value):
    return pltpu.with_memory_space_constraint(value, pltpu.HBM)


def in_vmem(value):
    return pltpu.with_memory_space_constraint(value, pltpu.VMEM)


def split_two(value):
    high = value.astype(BF16)
    low = (value - high.astype(F32)).astype(BF16)
    return high, low


def call(kernel, outs, in_specs, args, vmem, name, scratch=(), out_specs=None, cost=None):
    single = not isinstance(outs, (list, tuple))
    if out_specs is None:
        out_specs = VM if single else [VM] * len(outs)
    return pl.pallas_call(
        kernel,
        out_shape=outs,
        in_specs=in_specs,
        out_specs=out_specs,
        scratch_shapes=list(scratch),
        name=name,
        cost_estimate=cost,
        compiler_params=pltpu.CompilerParams(vmem_limit_bytes=vmem),
    )(*args)


def shape_of(shape, dtype):
    return jax.ShapeDtypeStruct(shape, dtype)


def first_rows_kernel(ids_ref, parents_ref, state_ref, *refs):
    out_refs, sem = refs[:-1], refs[-1]
    local_rows = state_ref.shape[0]
    both = 2 * local_rows
    me = ids_ref[0]
    copies = []
    for hop, out_ref in enumerate(out_refs, 1):
        to = ids_ref[2 * hop] // 2
        low = jnp.int32(local_rows)
        for i in range(both):
            parent = parents_ref[0, to * both + i]
            here = parent // local_rows == me
            low = jnp.where(here, jnp.minimum(low, lax.rem(parent, local_rows)), low)
        row = jnp.where(low < local_rows, low, 0)
        copies.append(pltpu.make_async_copy(state_ref.at[pl.ds(row, 1)], out_ref, sem.at[hop - 1]))
        copies[-1].start()
    for copy in copies:
        copy.wait()


def first_rows(targets, parents, state):
    count = targets.shape[0] // 2 - 1
    return call(
        first_rows_kernel,
        [pltpu.VMEM((1, *state.shape[1:]), BF16)] * count,
        [SM, SM, ANY],
        (targets, parents, in_hbm(state)),
        MIB,
        "first_rows",
        scratch=[pltpu.SemaphoreType.DMA((count,))],
    )


def in_load_kernel(
    tok_hbm, gain_hbm, dt_hbm, xz_hbm, lhs_ref, tail_ref, piece_ref, tok_ref, gain_ref, dt_ref, sem_small, sem
):
    rows, depth = tok_ref.shape
    heads = dt_hbm.shape[0]
    small = [
        pltpu.make_async_copy(tok_hbm, tok_ref, sem_small.at[0]),
        pltpu.make_async_copy(gain_hbm, gain_ref, sem_small.at[1]),
        pltpu.make_async_copy(dt_hbm, dt_ref.at[pl.ds(0, heads)], sem_small.at[2]),
    ]
    copies = [pltpu.make_async_copy(xz_hbm.at[:, t], piece_ref.at[t], sem.at[t]) for t in range(piece_ref.shape[0])]
    for one in small + copies:
        one.start()
    dt_ref[heads:, :] = jnp.zeros((LANES - heads, depth), BF16)
    small[0].wait()
    small[1].wait()
    inputs = tok_ref[...].astype(F32)
    squares = jnp.sum(inputs * inputs, axis=1, keepdims=True)
    scaled = (inputs * gain_ref[0:1, :]).astype(BF16)
    row = iota((LANES, 4 * LANES), 0)
    col = iota((LANES, 4 * LANES), 1)
    spread = one_hot((col == 2 * row) | (col == 2 * LANES + 2 * row + 1))
    blocks = depth // LANES
    stacked = jnp.concatenate([scaled[:, i * LANES : (i + 1) * LANES] for i in range(blocks)], axis=0)
    wide = dot(stacked, spread).astype(BF16)
    for i in range(blocks):
        where = slice(i * 2 * LANES, (i + 1) * 2 * LANES)
        block = wide[i * rows : (i + 1) * rows]
        lhs_ref[0:rows, where] = block[:, : 2 * LANES]
        lhs_ref[rows : 2 * rows, where] = block[:, 2 * LANES :]
    small[2].wait()
    tail = dot_t(scaled, dt_ref[...])
    high, low = split_two(squares)
    lane = iota(tail.shape, 1)
    tail = jnp.where(lane == heads, high.astype(F32), jnp.where(lane == heads + 1, low.astype(F32), tail))
    tail_ref[...] = tail.astype(BF16)
    for one in copies:
        one.wait()


def multiply_tiles(lhs, tiles_ref, store):
    count = tiles_ref.shape[0]
    step = 2 if count % 2 == 0 else 1
    for t in range(0, count, step):
        weights = tiles_ref[t] if step == 1 else jnp.concatenate([tiles_ref[t], tiles_ref[t + 1]], axis=1)
        store(t * LANES, step * LANES, dot(lhs, weights).astype(BF16))


def in_middle_kernel(lhs_ref, tiles_ref, xz_hbm, bc_hbm, out_ref, piece_ref, piece_bc_ref, sem, sem_bc):
    done = tiles_ref.shape[0]
    copies = [
        pltpu.make_async_copy(xz_hbm.at[:, done + t], piece_ref.at[t], sem.at[t]) for t in range(piece_ref.shape[0])
    ] + [pltpu.make_async_copy(bc_hbm.at[:, t], piece_bc_ref.at[t], sem_bc.at[t]) for t in range(piece_bc_ref.shape[0])]
    for one in copies:
        one.start()

    def store(start, width, product):
        out_ref[:, start : start + width] = product

    multiply_tiles(lhs_ref[...], tiles_ref, store)
    for one in copies:
        one.wait()


def in_last_kernel(lhs_ref, early_ref, tail_ref, tiles_ref, tiles_bc_ref, out_ref):
    rows = tail_ref.shape[0]
    before = early_ref.shape[1]
    inner = before + tiles_ref.shape[0] * LANES
    groups_width = tiles_bc_ref.shape[0] * LANES
    out_ref[:, 0:before] = early_ref[0:rows]
    out_ref[:, inner : inner + before] = early_ref[rows : 2 * rows]
    base = 2 * inner + 2 * groups_width
    out_ref[:, base : base + LANES] = tail_ref[...]

    def store_at(first, second):
        def store(start, width, product):
            out_ref[:, first + start : first + start + width] = product[0:rows]
            out_ref[:, second + start : second + start + width] = product[rows : 2 * rows]

        return store

    multiply_tiles(lhs_ref[...], tiles_ref, store_at(before, inner + before))
    multiply_tiles(lhs_ref[...], tiles_bc_ref, store_at(2 * inner, 2 * inner + groups_width))


def in_proj(tokens, gains, weight_xz, weight_bc, weight_dt):
    rows, depth = tokens.shape
    inner = weight_xz.shape[2]
    groups_width = weight_bc.shape[2]
    heads = weight_dt.shape[1]
    tiles, tiles_bc = inner // LANES, groups_width // LANES
    half = tiles // 2
    xz = weight_xz.reshape(depth, 2, tiles, LANES).transpose(0, 2, 1, 3)
    bc = weight_bc.reshape(depth, 2, tiles_bc, LANES).transpose(0, 2, 1, 3)
    width = 2 * inner + 2 * groups_width + LANES

    def flat(piece):
        return in_vmem(piece.reshape(piece.shape[0], 2 * depth, LANES))

    def piece_of(count):
        return pltpu.VMEM((count, depth, 2, LANES), BF16)

    lhs, tail, piece = call(
        in_load_kernel,
        [shape_of((2 * rows, 2 * depth), BF16), shape_of((rows, LANES), BF16), piece_of(half)],
        [ANY] * 4,
        [in_hbm(one) for one in (tokens, gains, weight_dt.T, xz)],
        6 * MIB,
        "in_load",
        scratch=[
            pltpu.VMEM((rows, depth), BF16),
            pltpu.VMEM(gains.shape, F32),
            pltpu.VMEM((LANES, depth), BF16),
            pltpu.SemaphoreType.DMA((3,)),
            pltpu.SemaphoreType.DMA((half,)),
        ],
        cost=moved(weight_xz.size),
    )
    early, piece, piece_bc = call(
        in_middle_kernel,
        [shape_of((2 * rows, half * LANES), BF16), piece_of(tiles - half), piece_of(tiles_bc)],
        [VM, VM, ANY, ANY],
        (lhs, flat(piece), in_hbm(xz), in_hbm(bc)),
        8 * MIB,
        "in_middle",
        scratch=[pltpu.SemaphoreType.DMA((tiles - half,)), pltpu.SemaphoreType.DMA((tiles_bc,))],
    )
    return call(
        in_last_kernel,
        shape_of((rows, width), BF16),
        [VM] * 5,
        (lhs, early, tail, flat(piece), flat(piece_bc)),
        8 * MIB,
        "in_last",
    )


def moved(size):
    return pl.CostEstimate(flops=0, bytes_accessed=2 * size, transcendentals=0)


def prefetch_kernel(from_ref, to_ref, sem):
    copy = pltpu.make_async_copy(from_ref, to_ref, sem)
    copy.start()
    copy.wait()


def prefetch(weight, after):
    weight, _ = lax.optimization_barrier((weight, after))
    return call(
        prefetch_kernel,
        pltpu.VMEM(weight.shape, BF16),
        [ANY],
        (in_hbm(weight),),
        MIB,
        "prefetch",
        scratch=[pltpu.SemaphoreType.DMA],
        cost=moved(2 * weight.size),
    )


def pick_rows_kernel(local_rows, capacity, slots, ids_ref, own_ref, other_ref, parents_ref, *out_refs):
    code_row, _ = codes(parents_ref, local_rows, capacity, slots)
    total = (own_ref[...].astype(F32) + other_ref[...].astype(F32)).astype(BF16)
    rows = total.shape[0]
    slot = iota((slots, rows), 0)
    for i, out_ref in enumerate(out_refs):
        pick = one_hot(code_row == ids_ref[i] * slots + slot)
        out_ref[...] = dot(pick, total).astype(BF16)


def pick_rows(targets, own, other, parents, local_rows, capacity, slots):
    width = own.shape[1]
    count = targets.shape[0]
    return call(
        functools.partial(pick_rows_kernel, local_rows, capacity, slots),
        [shape_of((slots, width), BF16)] * count,
        [SM, VM, VM, VM],
        (targets, own, other, parents),
        8 * MIB,
        "pick_rows",
    )


def chip_sum_kernel(own_ref, other_ref, out_ref):
    out_ref[...] = (own_ref[...].astype(F32) + other_ref[...].astype(F32)).astype(BF16)


def chip_sum(own, other):
    return call(chip_sum_kernel, shape_of(own.shape, BF16), [VM, VM], (own, other), 4 * MIB, "chip_sum")


def mixer_kernel(parts, heads, capacity, ids_ref, parents_ref, *refs):
    part_refs = refs[:parts]
    (
        conv_ref,
        conv_bc_ref,
        bias_ref,
        rates_ref,
        skip_ref,
        gain_ref,
        queue_ref,
        queue_bc_ref,
        state_hbm,
        act_ref,
        message_ref,
        state_ref,
        sem,
    ) = refs[parts:]
    fetched = [pltpu.make_async_copy(state_hbm.at[r], state_ref.at[r], sem.at[r]) for r in range(state_ref.shape[0])]
    for one in fetched:
        one.start()
    slots = part_refs[0].shape[0]
    inner = gain_ref.shape[1]
    lags, local_rows, _ = queue_ref.shape
    groups_width = queue_bc_ref.shape[3]
    state_size = state_ref.shape[3]
    head_size = state_ref.shape[2]
    groups_here = groups_width // state_size
    per_group = inner // groups_here
    proj = part_refs[0][...].astype(F32)
    for ref in part_refs[1:]:
        proj = proj + ref[...].astype(F32)
    base_bc = 2 * inner
    base = base_bc + 2 * groups_width
    tail = proj[:, base : base + LANES]
    lane = iota(tail.shape, 1)
    squares = jnp.sum(jnp.where((lane == heads) | (lane == heads + 1), tail, 0.0), axis=1, keepdims=True)
    scale = lax.rsqrt(squares / D + EPS)
    code_row, _ = codes(parents_ref, local_rows, capacity, slots)
    slot = iota((slots, code_row.shape[1]), 0)
    mine = code_row == ids_ref[0] * slots + slot
    valid = jnp.sum(jnp.where(mine, 1.0, 0.0), axis=1, keepdims=True)
    parent = jnp.sum(jnp.where(mine, lax.rem(parents_ref[...], local_rows), 0), axis=1, keepdims=True)
    pick = jnp.where((iota((slots, local_rows), 1) == parent) & (valid > 0.0), 1.0, 0.0).astype(BF16)

    now = proj[:, 0:inner] * scale
    gate = proj[:, inner : 2 * inner] * scale
    conv = now * conv_ref[lags : lags + 1, :]
    for k in range(lags):
        held = dot(pick, queue_ref[k])
        conv = conv + held * conv_ref[k : k + 1, :]
        if k > 0:
            message_ref[:, (k - 1) * inner : k * inner] = held.astype(BF16)
    message_ref[:, (lags - 1) * inner : lags * inner] = now.astype(BF16)
    inner_vals = conv * jax.nn.sigmoid(conv)
    at = lags * inner
    keys = []
    for j in range(2):
        start = base_bc + j * groups_width
        now_bc = proj[:, start : start + groups_width] * scale
        conv_bc = now_bc * conv_bc_ref[lags, j : j + 1, :]
        for k in range(lags):
            held = dot(pick, queue_bc_ref[k, j])
            conv_bc = conv_bc + held * conv_bc_ref[k, j : j + 1, :]
            if k > 0:
                to = at + ((k - 1) * 2 + j) * groups_width
                message_ref[:, to : to + groups_width] = held.astype(BF16)
        to = at + ((lags - 1) * 2 + j) * groups_width
        message_ref[:, to : to + groups_width] = now_bc.astype(BF16)
        keys.append(conv_bc * jax.nn.sigmoid(conv_bc))
    at = at + lags * 2 * groups_width

    raw = tail * scale + bias_ref[...]
    steps = jnp.maximum(raw, 0.0) + jnp.log1p(jnp.exp(-jnp.abs(raw)))
    decays = jnp.exp(-steps * rates_ref[...])
    spread = one_hot(iota((LANES, inner), 0) == iota((LANES, inner), 1) // head_size)

    def expand(value):
        high, low = split_two(value)
        return dot(high, spread) + dot(low, spread)

    steps_wide = expand(steps)
    decays_wide = expand(decays)
    skip_wide = expand(jnp.broadcast_to(skip_ref[...], (8, LANES)))[0:1]
    update = steps_wide * inner_vals
    message_ref[:, at : at + inner] = update.astype(BF16)
    at = at + inner
    message_ref[:, at : at + groups_width] = keys[0].astype(BF16)
    at = at + groups_width
    decay_high, decay_low = split_two(decays)
    message_ref[:, at : at + LANES] = decay_high
    message_ref[:, at + LANES : at + 2 * LANES] = decay_low

    for g in range(groups_here):
        lanes = slice(g * state_size, (g + 1) * state_size)
        wide = slice(g * per_group, (g + 1) * per_group)
        b_vals, c_vals = keys[0][:, lanes], keys[1][:, lanes]
        high, low = split_two(c_vals)
        c_both = jnp.concatenate([high, low], axis=0)
        mixed = jnp.zeros((slots, per_group), F32)
        first_head = g * (per_group // head_size)
        for r in range(local_rows):
            if g == 0:
                fetched[r].wait()
            block = state_ref[r, first_head : first_head + per_group // head_size]
            both = dot_t(c_both, block.reshape(per_group, state_size))
            mixed = mixed + jnp.where(parent == r, both[0:slots] + both[slots : 2 * slots], 0.0)
        inside = jnp.sum(b_vals * c_vals, axis=1, keepdims=True)
        mixed = decays_wide[:, wide] * mixed + update[:, wide] * inside + skip_wide[:, wide] * inner_vals[:, wide]
        gated = mixed * (gate[:, wide] * jax.nn.sigmoid(gate[:, wide]))
        mean = jnp.sum(gated * gated, axis=1, keepdims=True) / per_group
        out = gated * lax.rsqrt(mean + EPS) * gain_ref[:, wide]
        act_ref[:, wide] = jnp.where(valid > 0.0, out, 0.0).astype(BF16)


def mixer(ids, parents, capacity, parts, params, queue, queue_bc, state):
    conv, conv_bc, bias, rates, skip, gain = params
    slots = parts[0].shape[0]
    inner = gain.shape[0]
    lags = queue.shape[0]
    groups_width = queue_bc.shape[3]
    heads = bias.shape[0]
    message = lags * (inner + 2 * groups_width) + inner + groups_width + 2 * LANES

    def lane_row(vector):
        return jnp.pad(vector, (0, LANES - heads)).reshape(1, LANES)

    return call(
        functools.partial(mixer_kernel, len(parts), heads, capacity),
        [shape_of((slots, inner), BF16), shape_of((slots, message), BF16)],
        [SM, VM] + [VM] * len(parts) + [VM] * 8 + [ANY],
        (ids, parents, *parts, conv, conv_bc, lane_row(bias), lane_row(rates), lane_row(skip), gain.reshape(1, inner), queue, queue_bc, in_hbm(state)),
        10 * MIB,
        "mixer",
        scratch=[pltpu.VMEM(state.shape, BF16), pltpu.SemaphoreType.DMA((state.shape[0],))],
    )


def deal_kernel(capacity, ids_ref, message_ref, *out_refs):
    slots = message_ref.shape[0]
    count = len(out_refs)
    row = iota((slots, slots), 0)
    want = row
    for i in range(slots // capacity):
        want = jnp.where(row // capacity == i, ids_ref[i] * capacity + row % capacity, want)
    order = one_hot(iota((slots, slots), 1) == want)
    dealt = dot(order, message_ref[...])
    at = 0
    for out_ref in out_refs:
        size = out_ref.shape[0]
        out_ref[...] = dealt[at : at + size].astype(BF16)
        at += size


def deal(targets, message, capacity):
    sizes = [capacity, capacity] + [2 * capacity] * (targets.shape[0] // 2 - 1)
    return call(
        functools.partial(deal_kernel, capacity),
        [shape_of((size, message.shape[1]), BF16) for size in sizes],
        [SM, VM],
        (targets, message),
        8 * MIB,
        "deal",
    )


def collect_kernel(rows, capacity, slots, lags, groups_width, ids_ref, parents_ref, *refs):
    in_refs, (inner_ref, groups_ref, update_ref, keys_ref, decay_ref) = refs[:-5], refs[-5:]
    count = len(in_refs)
    code_row, code_col = codes(parents_ref, rows, capacity, slots)
    everyone = code_col.shape[0]
    inner = update_ref.shape[1]
    me = ids_ref[0]
    parts = []
    for i, ref in enumerate(in_refs):
        value = ref[...].astype(F32)
        start = capacity if i > 1 and i % 2 else 0
        parts.append(value[start : start + capacity])
    held = jnp.concatenate(parts, axis=0).astype(BF16)
    col = iota((everyone, count * capacity), 1)
    want = jnp.full(col.shape, -1, jnp.int32)
    for i in range(count):
        want = jnp.where(col // capacity == i, ids_ref[i] * slots + me * capacity + col % capacity, want)
    chosen = one_hot(code_col == want)
    here = one_hot(iota((rows, everyone), 1) == me * rows + iota((rows, everyone), 0))
    mine = dot(dot(here, chosen).astype(BF16), held)
    for k in range(lags):
        inner_ref[k] = mine[:, k * inner : (k + 1) * inner].astype(BF16)
    at = lags * inner
    for k in range(lags):
        for j in range(2):
            start = at + (2 * k + j) * groups_width
            groups_ref[:, k, j, :] = mine[:, start : start + groups_width].astype(BF16)
    at = at + 2 * lags * groups_width
    update_ref[...] = mine[:, at : at + inner]
    at = at + inner
    keys_ref[...] = mine[:, at : at + groups_width]
    at = at + groups_width
    decay_ref[...] = mine[:, at : at + LANES] + mine[:, at + LANES : at + 2 * LANES]


def collect(sources, parents, rows, messages, slots, inner, groups_width, lags):
    capacity = messages[0].shape[0]
    return call(
        functools.partial(collect_kernel, rows, capacity, slots, lags, groups_width),
        [
            shape_of((lags, rows, inner), BF16),
            shape_of((rows, lags, 2, groups_width), BF16),
            shape_of((rows, inner), F32),
            shape_of((rows, groups_width), F32),
            shape_of((rows, LANES), F32),
        ],
        [SM, VM] + [VM] * len(messages),
        (sources, parents, *messages),
        8 * MIB,
        "collect",
    )


def fetch_row(entry, local_rows, kinds, refs, to, sem):
    kind = entry // local_rows
    row = lax.rem(entry, local_rows)
    for known, ref in zip(kinds, refs):

        @pl.when(kind == known)
        def _(ref=ref):
            pltpu.make_async_copy(ref.at[pl.ds(row, 1)], to, sem).start()


def gather_kernel(local_rows, kinds, table_ref, *refs):
    count = len(kinds)
    in_refs, out_refs, sem = refs[:count], refs[count:-1], refs[-1]
    places = [(ref, i) for ref in out_refs for i in range(ref.shape[0])]
    for j, (ref, i) in enumerate(places):
        fetch_row(table_ref[j], local_rows, kinds, in_refs, ref.at[pl.ds(i, 1)], sem.at[j])
    for j, (ref, i) in enumerate(places):
        pltpu.make_async_copy(in_refs[0].at[pl.ds(0, 1)], ref.at[pl.ds(i, 1)], sem.at[j]).wait()


def gather_rows(table, states, sizes):
    shape = states[0].shape
    return call(
        functools.partial(gather_kernel, shape[0], tuple(range(len(states)))),
        [pltpu.VMEM((size, *shape[1:]), BF16) for size in sizes],
        [SM] + [ANY] * len(states),
        (table, in_hbm(states[0]), *states[1:]),
        MIB,
        "gather_rows",
        scratch=[pltpu.SemaphoreType.DMA((sum(sizes),))],
    )


def update_kernel(kinds, is_mine, table_ref, *refs):
    sources = len(kinds)
    state_refs = refs[:sources]
    update_ref, keys_ref, decay_ref = refs[sources : sources + 3]
    out_ref, held, made, sem_in, sem_out = refs[-5:]
    rows, heads, head_size, state_size = held.shape
    inner = update_ref.shape[1]
    groups_here = keys_ref.shape[1] // state_size
    per_group = inner // groups_here
    heads_group = heads // groups_here

    mine = [is_mine(table_ref[j] // rows) for j in range(rows)]
    for j in range(rows):

        @pl.when(mine[j])
        def _(j=j):
            fetch_row(table_ref[j], rows, kinds, state_refs, held.at[pl.ds(j, 1)], sem_in.at[j])

    spread = one_hot(iota((LANES, inner), 0) == iota((LANES, inner), 1) // head_size)
    high, low = split_two(decay_ref[...])
    decay_high, decay_low = dot(high, spread), dot(low, spread)
    columns = []
    for g in range(groups_here):
        wide = slice(g * per_group, (g + 1) * per_group)
        stacked = jnp.concatenate([update_ref[:, wide], decay_high[:, wide], decay_low[:, wide]], axis=0)
        columns.append(jnp.transpose(stacked).astype(BF16))
    row_id = iota((3 * rows, state_size), 0)
    def renew(j):
        pltpu.make_async_copy(state_refs[0].at[pl.ds(0, 1)], held.at[pl.ds(j, 1)], sem_in.at[j]).wait()
        for g in range(groups_here):
            keys = keys_ref[j : j + 1, g * state_size : (g + 1) * state_size]
            right_keys = jnp.where(row_id == j, keys, 0.0)
            right_ones = jnp.where((row_id == rows + j) | (row_id == 2 * rows + j), 1.0, 0.0)
            right = jnp.concatenate([right_keys, right_ones], axis=1).astype(BF16)
            both = dot(columns[g], right)
            which = slice(g * heads_group, (g + 1) * heads_group)
            before = held[j, which].reshape(per_group, state_size).astype(F32)
            after = both[:, state_size:] * before + both[:, :state_size]
            made[j, which] = after.astype(BF16).reshape(heads_group, head_size, state_size)
        pltpu.make_async_copy(made.at[j], out_ref.at[j], sem_out.at[j]).start()

    for j in range(rows):
        pl.when(mine[j])(functools.partial(renew, j))
    for j in range(rows):

        @pl.when(mine[j])
        def _(j=j):
            pltpu.make_async_copy(made.at[j], out_ref.at[j], sem_out.at[j]).wait()


def update_state(table, states, update, keys, decay, is_mine, before=None):
    kinds = tuple(sorted(states))
    shape = states[0].shape
    args = [table, in_hbm(states[0]), *[states[kind] for kind in kinds[1:]], update, keys, decay]
    specs = [SM] + [ANY] * len(kinds) + [VM] * 3
    aliases = {}
    if before is not None:
        aliases = {len(args): 0}
        args.append(in_hbm(before))
        specs.append(pl.BlockSpec(memory_space=pltpu.HBM))
    return pl.pallas_call(
        functools.partial(update_kernel, kinds, is_mine),
        out_shape=pltpu.HBM(shape, BF16),
        in_specs=specs,
        out_specs=pl.BlockSpec(memory_space=pltpu.HBM),
        scratch_shapes=[
            pltpu.VMEM(shape, BF16),
            pltpu.VMEM(shape, BF16),
            pltpu.SemaphoreType.DMA((shape[0],)),
            pltpu.SemaphoreType.DMA((shape[0],)),
        ],
        input_output_aliases=aliases,
        name="update_state",
        compiler_params=pltpu.CompilerParams(vmem_limit_bytes=16 * MIB),
    )(*args)


def no_rows_kernel(*refs):
    pass


def no_rows(shape, count):
    return pl.pallas_call(
        no_rows_kernel,
        out_shape=[pltpu.HBM(shape, BF16)] * count,
        out_specs=[pl.BlockSpec(memory_space=pltpu.HBM)] * count,
        name="no_rows",
    )()


def fetch_pieces(from_ref, to_ref, sem):
    count = sem.shape[0]
    depth = to_ref.shape[0] // count
    pieces = []
    for i in range(count):
        piece = pl.ds(i * depth, depth)
        copy = pltpu.make_async_copy(from_ref.at[piece], to_ref.at[piece], sem.at[i])
        copy.start()
        pieces.append((slice(i * depth, (i + 1) * depth), copy))
    return pieces


def multiply_pieces(left, weight_ref, pieces):
    total = None
    for piece, copy in pieces:
        copy.wait()
        product = dot(left[:, piece], weight_ref[piece, :])
        total = product if total is None else total + product
    return total


def out_proj_kernel(local_rows, capacity, slots, ids_ref, parents_ref, *refs):
    act_refs, (weight_hbm, out_ref, weight_ref, sem) = refs[:-4], refs[-4:]
    pieces = fetch_pieces(weight_hbm, weight_ref, sem)
    _, code_col = codes(parents_ref, local_rows, capacity, slots)
    rows = code_col.shape[0]
    devices = len(act_refs)
    col = iota((rows, devices * slots), 1)
    want = jnp.full(col.shape, -1, jnp.int32)
    for i in range(devices):
        want = jnp.where(col // slots == i, ids_ref[i] * slots + col % slots, want)
    held = jnp.concatenate([ref[...] for ref in act_refs], axis=0)
    activity = dot(one_hot(code_col == want), held).astype(BF16)
    out_ref[...] = multiply_pieces(activity, weight_ref, pieces).astype(BF16)


def out_proj(sources, parents, local_rows, capacity, acts, weight):
    rows = parents.shape[1]
    return call(
        functools.partial(out_proj_kernel, local_rows, capacity, acts[0].shape[0]),
        shape_of((rows, weight.shape[1]), BF16),
        [SM, VM] + [VM] * len(acts) + [ANY],
        (sources, parents, *acts, in_hbm(weight)),
        12 * MIB,
        "out_proj",
        scratch=[pltpu.VMEM(weight.shape, BF16), pltpu.SemaphoreType.DMA((4,))],
    )


def up_kernel(parts, tok_ref, gain_ref, *refs):
    part_refs = refs[:parts]
    weight_ref, residual_ref, out_ref = refs[parts:]
    residual = tok_ref[...].astype(F32)
    total = part_refs[0][...].astype(F32)
    for ref in part_refs[1:]:
        total = total + ref[...].astype(F32)
    residual = residual + total
    residual_ref[...] = residual
    squares = jnp.sum(residual * residual, axis=1, keepdims=True)
    scaled = (residual * gain_ref[1:2, :]).astype(BF16)
    width = weight_ref.shape[1]
    high, low = split_two(squares)
    lane = iota((scaled.shape[0], LANES), 1)
    out_ref[:, width : width + LANES] = jnp.where(
        lane == 0, high.astype(F32), jnp.where(lane == 1, low.astype(F32), 0.0)
    ).astype(BF16)
    out_ref[:, 0:width] = dot(scaled, weight_ref[...]).astype(BF16)


def up_proj(tokens, gains, parts, weight):
    rows, width = tokens.shape
    return call(
        functools.partial(up_kernel, len(parts)),
        [shape_of((rows, width), F32), shape_of((rows, weight.shape[1] + LANES), BF16)],
        [VM] * (len(parts) + 3),
        (tokens, gains, *parts, in_vmem(weight)),
        8 * MIB,
        "up_proj",
    )


def down_kernel(*refs):
    part_refs, (weight_hbm, out_ref, weight_ref, sem) = refs[:-4], refs[-4:]
    pieces = fetch_pieces(weight_hbm, weight_ref, sem)
    total = part_refs[0][...].astype(F32)
    for ref in part_refs[1:]:
        total = total + ref[...].astype(F32)
    width = weight_ref.shape[0]
    squares = jnp.sum(total[:, width : width + LANES], axis=1, keepdims=True)
    hidden = jnp.maximum(total[:, 0:width] * lax.rsqrt(squares / D + EPS), 0.0)
    out_ref[...] = multiply_pieces((hidden * hidden).astype(BF16), weight_ref, pieces).astype(BF16)


def down_proj(parts, weight):
    rows = parts[0].shape[0]
    return call(
        down_kernel,
        shape_of((rows, weight.shape[1]), BF16),
        [VM] * len(parts) + [ANY],
        (*parts, in_hbm(weight)),
        20 * MIB,
        "down_proj",
        scratch=[pltpu.VMEM(weight.shape, BF16), pltpu.SemaphoreType.DMA((8,))],
    )


def finish_kernel(residual_ref, *refs):
    part_refs, out_ref = refs[:-1], refs[-1]
    total = part_refs[0][...].astype(F32)
    for ref in part_refs[1:]:
        total = total + ref[...].astype(F32)
    out_ref[0] = (residual_ref[...] + total).astype(BF16)


def finish(residual, parts):
    return call(
        finish_kernel,
        shape_of((1, *residual.shape), BF16),
        [VM] * (len(parts) + 1),
        (residual, *parts),
        6 * MIB,
        "finish",
    )


def plan_rows(chosen, chips, local_rows):
    rows = chosen.shape[0]
    both = 2 * local_rows
    same = chosen[:, None] == jnp.arange(rows, dtype=jnp.int32)[None, :]
    needed = jnp.any(same.reshape(chips, both, rows), axis=1).reshape(chips, chips, 2, local_rows)
    small = jnp.arange(local_rows, dtype=jnp.int32)
    before = jnp.sum(jnp.where(small[None, :] < small[:, None], needed[:, :, :, None, :], False), axis=4)
    first = (needed & (before == 0)).reshape(chips, chips, both)
    needed = needed.reshape(chips, chips, both)
    rest = needed & ~first
    wide = jnp.arange(both, dtype=jnp.int32)
    rank = jnp.sum(jnp.where(wide[None, :] < wide[:, None], rest[:, :, None, :], False), axis=3)
    lane = jnp.where(first, wide // local_rows, rank % 2)
    turn = jnp.where(first, 0, 1 + rank // 2)
    return needed, lane.astype(jnp.int32), turn.astype(jnp.int32)


def rounds_of(chosen, chips, local_rows):
    rows = chosen.shape[0]
    same = chosen[:, None] == jnp.arange(rows, dtype=jnp.int32)[None, :]
    needed = jnp.any(same.reshape(chips, 2 * local_rows, rows), axis=1).reshape(chips, chips, 2, local_rows)
    counts = jnp.sum(needed, axis=3).astype(jnp.int32)
    rest = jnp.sum(counts - jnp.minimum(counts, 1), axis=2)
    apart = jnp.arange(chips)[:, None] != jnp.arange(chips)[None, :]
    return jnp.max(jnp.where(apart, 1 + (rest + 1) // 2, 0))


def on_device(
    tokens,
    parents,
    norm_gains,
    weight_xz,
    weight_bc,
    weight_dt,
    conv_inner,
    conv_groups,
    dt_bias,
    rates,
    skip_gain,
    gate_gain,
    weight_out,
    weight_up,
    weight_down,
    ssm_state,
    queue_inner,
    queue_groups,
):
    devices = lax.axis_size("dp")
    chips = devices // 2
    ranks = lax.axis_size("tensor")
    me = lax.axis_index("dp")
    chip, core = me // 2, me % 2
    local_rows = ssm_state.shape[0]
    lags = queue_inner.shape[1]
    inner = queue_inner.shape[2]
    groups_width = queue_groups.shape[3]
    capacity = max(2, 2 * local_rows // devices)
    slots = devices * capacity
    rows = parents.shape[1]
    barrier = lax.optimization_barrier

    def to_dp(value, hop, flip):
        pairs = [(i, ((i // 2 + hop) % chips) * 2 + ((i % 2) ^ flip)) for i in range(devices)]
        return lax.ppermute(value, "dp", pairs)

    def over_tensor(value):
        return [value] + [
            lax.ppermute(value, "tensor", [(i, (i + s) % ranks) for i in range(ranks)]) for s in range(1, ranks)
        ]

    hops = [(hop, flip) for hop in range(chips) for flip in range(2)]
    sources = jnp.stack([((chip + chips - hop) % chips) * 2 + (core ^ flip) for hop, flip in hops]).astype(jnp.int32)
    targets = jnp.stack([((chip + hop) % chips) * 2 + (core ^ flip) for hop, flip in hops]).astype(jnp.int32)

    chosen = parents[0]
    place = jnp.arange(rows, dtype=jnp.int32)

    def after(value, *earlier):
        return barrier((value, *earlier))[0]

    sibling_state = to_dp(ssm_state, 0, 1)
    states = {0: ssm_state, 1: sibling_state}
    first_sent = first_rows(targets, parents, ssm_state)
    first = [to_dp(buffer, hop, 0) for hop, buffer in enumerate(first_sent, 1)]
    partial = in_proj(after(tokens[0], *first_sent), norm_gains, weight_xz, weight_bc, weight_dt)

    near = to_dp(partial, 0, 1)
    most = min(2 * local_rows, 4 * capacity)
    turns = 1 + (max(min(most, local_rows) - 1, most - 2) + 1) // 2
    early = min(turns, max(3, (turns + 2) // 2))
    single = min(3, early)
    near, *first = barrier((near, *first))
    picked = pick_rows(targets[0::2], partial, near, parents, local_rows, capacity, slots)
    needed, lane, turn = plan_rows(after(chosen, picked[0]), chips, local_rows)
    chip_rows = jnp.arange(2 * local_rows, dtype=jnp.int32)
    entries = ((chip_rows // local_rows) ^ core) * local_rows + chip_rows % local_rows
    send_tables = []
    for hop in range(1, chips):
        to = (chip + hop) % chips
        mine = needed[to, chip] & (lane[to, chip] == core)
        at_turn = mine[None, :] & (turn[to, chip][None, :] == jnp.arange(turns, dtype=jnp.int32)[:, None])
        send_tables.append(jnp.sum(jnp.where(at_turn, entries[None, :], 0), axis=1).astype(jnp.int32))

    def where_from():
        own_chosen = lax.dynamic_slice_in_dim(chosen, me * local_rows, local_rows, 0)
        parent_chip = own_chosen // (2 * local_rows)
        lookup = own_chosen[:, None] == place[None, :]
        lane_of = jnp.sum(jnp.where(lookup, lane[chip].reshape(1, rows), 0), axis=1)
        turn_of = jnp.sum(jnp.where(lookup, turn[chip].reshape(1, rows), 0), axis=1)
        hop_of = (chip + chips - parent_chip) % chips
        here = ((own_chosen // local_rows) % 2) ^ core
        start_of = jnp.where(turn_of >= early, early, jnp.minimum(turn_of, single))
        there = 2 + ((hop_of - 1) * 2 + (lane_of ^ core)) * turns + start_of
        inside = jnp.where(parent_chip == chip, own_chosen % local_rows, turn_of - start_of)
        return (jnp.where(parent_chip == chip, here, there) * local_rows + inside).astype(jnp.int32)

    def kind_of(hop, at):
        return 2 + (hop - 1) * 2 * turns + at

    parts = [picked[0]] + [to_dp(picked[hop], hop, 0) for hop in range(1, chips)]

    waiting = []
    sizes = [1] * (single - 1) + [early - single] * (early > single)
    for hop in range(1, chips):
        wanted = after(send_tables[hop - 1][1:early], picked[0])
        waiting.append(gather_rows(wanted, [ssm_state, sibling_state], sizes))
    table = where_from()
    parts[0] = after(parts[0], table, *[some[0] for some in waiting])
    act, message = mixer(
        sources,
        parents,
        capacity,
        parts,
        (conv_inner, conv_groups, dt_bias, rates, skip_gain, gate_gain),
        queue_inner.transpose(1, 0, 2),
        queue_groups.transpose(1, 2, 0, 3),
        ssm_state,
    )
    acts = [act] + [to_dp(act, hop, flip) for hop, flip in hops[1:]]
    arrived, relayed = {0: first}, {}

    def relay(at, *earlier):
        relayed[at] = [to_dp(after(some, *earlier), 0, 1) for some in arrived[at]]

    relay(0, act)
    acts[0], relayed[0] = barrier((acts[0], relayed[0]))


    def send_turn(at, *earlier):
        return [to_dp(after(some[at - 1], *earlier), hop, 0) for hop, some in enumerate(waiting, 1)]

    out_part = out_proj(sources, parents, local_rows, capacity, acts, weight_out)
    arrived[1] = send_turn(1, *acts)
    out_parts = over_tensor(out_part)
    for at in range(2, single):
        arrived[at] = send_turn(at, out_part)
    weight_up = prefetch(weight_up, out_part)
    dealt = deal(targets, after(message, weight_up), capacity)
    out_parts[0], arrived[1], *dealt = barrier((out_parts[0], arrived[1], *dealt))
    residual, up_part = up_proj(tokens[0], norm_gains, out_parts, weight_up)
    sent = [to_dp(after(dealt[1 + hop], up_part), hop, 0) for hop in range(1, chips)]
    between = {at: arrived[at] for at in range(2, single)}
    near_up, between = barrier((to_dp(up_part, 0, 1), between))
    arrived.update(between)
    up_chip = chip_sum(up_part, near_up)
    up_parts = [up_chip] + [to_dp(up_chip, hop, 0) for hop in range(1, chips)]

    for at in range(1, single):
        relay(at, up_chip)
    messages = [dealt[0], to_dp(after(dealt[1], up_chip), 0, 1)]
    for some in sent:
        messages += [some, to_dp(after(some, up_chip), 0, 1)]
    final_inner, final_groups, update, keys, decay = collect(
        sources, parents, local_rows, messages, slots, inner, groups_width, lags
    )
    chosen = after(chosen, update)
    groups = lax.axis_size("groups")
    longest = rounds_of(chosen, chips, local_rows)
    for shift in range(1, groups):
        other = lax.ppermute(chosen, "groups", [(i, (i + shift) % groups) for i in range(groups)])
        longest = jnp.maximum(longest, rounds_of(other, chips, local_rows))
    up_parts[0], relayed, update = barrier((up_parts[0], relayed, update))
    if early > single:
        arrived[single] = send_turn(single, *up_parts)
    down_part = down_proj(up_parts, weight_down)
    down_parts = over_tensor(down_part)

    def is_early(kind):
        return (kind < 2) | (lax.rem(kind - 2, turns) < single)

    def is_late(kind):
        return jnp.logical_not(is_early(kind))

    def add_states(turn_range):
        for at in turn_range:
            for hop in range(1, chips):
                states[kind_of(hop, at)] = arrived[at][hop - 1]
                states[kind_of(hop, at) + turns] = relayed[at][hop - 1]

    add_states(range(single))
    final_state = update_state(table, states, update, keys, decay, is_early)
    residual, final_state, longest = barrier((residual, final_state, longest))
    beam_out = finish(residual, down_parts)
    if early > single:
        relay(single, final_state)
        add_states([single])

    more = (turns - early, *ssm_state.shape[1:])

    def fetch_more():
        fetched = []
        for hop in range(1, chips):
            wanted = send_tables[hop - 1][early:]
            (buffer,) = gather_rows(wanted, [ssm_state, sibling_state], [turns - early])
            fetched.append(to_dp(buffer, hop, 0))
            fetched.append(to_dp(fetched[-1], 0, 1))
        return tuple(fetched)

    fetched = []
    if turns > early:
        fetched = lax.cond(longest > early, fetch_more, lambda: tuple(no_rows(more, 2 * (chips - 1))))
    late_states = {0: ssm_state}
    for hop in range(1, chips):
        if turns > early:
            late_states[kind_of(hop, early)] = fetched[2 * hop - 2]
            late_states[kind_of(hop, early) + turns] = fetched[2 * hop - 1]
        if early > single:
            for kind in (kind_of(hop, single), kind_of(hop, single) + turns):
                late_states[kind] = states[kind]
    final_state = update_state(table, late_states, update, keys, decay, is_late, final_state)
    return (beam_out, final_state, final_inner.transpose(1, 0, 2), final_groups)


def solution(mesh):
    in_specs = (
        P(None, "groups", "dp"),
        P(None, "groups"),
        P(None, "dp"),
        P("dp", None, "tensor"),
        P("dp", None, "tensor"),
        P("dp", "tensor"),
        P(None, "tensor"),
        P(None, None, "tensor"),
        P("tensor"),
        P("tensor"),
        P("tensor"),
        P("tensor"),
        P("tensor", "dp"),
        P("dp", "tensor"),
        P("tensor", "dp"),
        P(("groups", "dp"), "tensor", None, None),
        P(("groups", "dp"), None, "tensor"),
        P(("groups", "dp"), None, None, "tensor"),
    )
    out_specs = (
        P(None, "groups", "dp"),
        P(("groups", "dp"), "tensor", None, None),
        P(("groups", "dp"), None, "tensor"),
        P(("groups", "dp"), None, None, "tensor"),
    )
    return jax.shard_map(
        on_device, mesh=mesh, in_specs=in_specs, out_specs=out_specs, check_vma=False
    )
```
